256 devices in a mesh: section: 2 (over x_hi), cp: 32 (over x_lo, z, core), fold: 4 (over y).
Axes of the slice: x: 4 (x_hi: 2, x_lo: 2; x = x_hi * 2 + x_lo), y: 4, z: 8, core: 2. Of those that a mesh axis runs over, the one named last changes fastest.
Arguments:
- activations: bfloat16 [2, 4096, 4096], P('section', 'cp', 'fold'), may hold values from -4 to 4
- queries: bfloat16 [2, 4096, 4096], P('section', 'cp', 'fold'), may hold values from -150 to 150
- keys: bfloat16 [2, 4096, 512], P('section', 'cp', 'fold'), may hold values from -6 to 6
- values: bfloat16 [2, 4096, 512], P('section', 'cp', 'fold'), may hold values from -6 to 6
- segments: int32 [2, 4096], P('section', 'cp'), may hold values from 0 to 7, never falling along the last dimension, each value on 1 to 2048 neighbouring positions
- routes: int32 [2, 4096, 8], P('section', 'cp'), may hold values from 0 to 63, all different within a row; in each aligned block of 128 rows (0 to 127, 128 to 255, ..., all dimensions but the last counted through in order) at most 20 rows name the same one
- route_weight: float32 [2, 4096, 8], P('section', 'cp'), may hold values from 0.1 to 1
- norm_gain: bfloat16 [2, 4096], P('section', 'fold'), may hold values from 0.25 to 4
- w_out: bfloat16 [2, 4096, 4096], P('section', 'fold', 'cp'), may hold values from -0.1875 to 0.1875
- w_gate: bfloat16 [2, 64, 768, 4096], P('section', 'cp', 'fold'), may hold values from -0.09375 to 0.09375
- w_up: bfloat16 [2, 64, 768, 4096], P('section', 'cp', 'fold'), may hold values from -0.09375 to 0.09375
- w_down: bfloat16 [2, 64, 768, 4096], P('section', 'cp', None, 'fold'), may hold values from -0.21875 to 0.21875
Outputs:
- passed: bfloat16 [2, 4096, 4096], P('section', 'cp', 'fold')
- passed_segments: int32 [2, 4096], P('section', 'cp')
The draws below stay inside these ranges and needn't reach their ends.
Inputs may be any that keep to these rules, and one draw needn't show every extreme that they name: `routes`: within the tokens of one index of cp of one section (aligned blocks of 128 rows), no expert is named more than 20 times, a bound that some block reaches. `segments`: document ids never fall along a section's tokens; a document has at most 2048 tokens.
All inputs are finite; a program needn't handle non-finite values.
Results may differ from the reference program's by a relative error of at most 0.02.
Values may be sent and summed in bfloat16 or wider, within the bound.
A program may use at most 128 MiB of HBM per device.

```python
import math
import jax
import jax.numpy as jnp
import numpy as np
from jax import lax

D = 4096
QUERY_HEADS = 32
KEY_VALUE_HEADS = 4
HEAD_SIZE = 128
HID = 768
TOPK = 8
DOCS = 8
TOK_DEV = 128
SECTION_TOKENS = 4096
EXPERTS = 64
CAP = 20
N_SECTION = 2


def shared_base(key):
    return jnp.clip(jax.random.normal(key, (N_SECTION, SECTION_TOKENS, KEY_VALUE_HEADS * HEAD_SIZE), jnp.float32), -6.0, 6.0)


def draw_keys(key, part):
    base_offset = shared_base(key)
    return base_offset.astype(jnp.bfloat16)


def draw_queries(key, part):
    key = jax.random.fold_in(key, 12)
    fresh = jnp.clip(jax.random.normal(key, (N_SECTION, SECTION_TOKENS, QUERY_HEADS, HEAD_SIZE), jnp.float32), -6.0, 6.0)
    return fresh.reshape(N_SECTION, SECTION_TOKENS, QUERY_HEADS * HEAD_SIZE).astype(jnp.bfloat16)


def strengthened(entries, stream_key, source, target, shards_of, factor):
    def block_of(position):
        return (jnp.arange(entries.shape[position]) // (entries.shape[position] // shards_of)).reshape((-1,) + (1,) * (entries.ndim - 1 - position))

    near = jax.random.permutation(stream_key, shards_of)[block_of(target)]
    other_side = (block_of(target) + shards_of // 2) % shards_of
    return jnp.where((block_of(source) == near) | (block_of(source) == other_side), factor * entries, entries)


def shard_levels(stream_key, dims, shards, low, top_value):
    level, own = 1.0, jax.random.fold_in(stream_key, 6)
    for position, shards_of in shards:
        heights = jnp.exp(jax.random.uniform(jax.random.fold_in(own, position), (shards_of,), jnp.float32, low / len(shards), top_value / len(shards)))
        level = level * jnp.repeat(heights, dims[position] // shards_of).reshape([-1 if axis == position else 1 for axis in range(len(dims))])
    return level


def profile(count, total, bound, lean):
    portions = [(1 << 20) // math.isqrt(grade ** lean) + 1 for grade in range(2, count + 1)]
    rest, holding = total - bound - (count - 1), [1] * (count - 1)
    while rest > 0:
        movable = [i for i in range(count - 1) if holding[i] < bound]
        mass, remaining = sum([portions[i] for i in movable]), rest
        for i in movable:
            more = min(bound - holding[i], max(1, remaining * portions[i] // mass), rest)
            holding[i] = holding[i] + more
            rest = rest - more
    return np.array([bound] + holding)


def uneven(stream_key, count, total, reach, skew):
    if count == 2:
        one = jax.random.randint(stream_key, (), max(1, total - reach), min(reach, total - 1) + 1)
        return jnp.stack([one, total - one])
    sizes = jnp.asarray(profile(count, total, reach, skew), jnp.int32)
    twos = (count - 1) // 2
    source_of, sink = sizes[1:1 + 2 * twos:2], sizes[2:2 + 2 * twos:2]
    margin = jnp.minimum(source_of - 1, reach - sink)
    moved = jax.random.randint(jax.random.fold_in(stream_key, 1), (twos,), 0, 1 << 20) % (margin + 1)
    sizes = sizes.at[1:1 + 2 * twos:2].set(source_of - moved).at[2:2 + 2 * twos:2].set(sink + moved)
    return sizes[jax.random.permutation(jax.random.fold_in(stream_key, 2), count)]


def shared_out(own_key, own, number, rows, count, top, limit, slope):
    sequence = jax.random.permutation(own_key, count)
    heavy_load, common = shares(count, rows * top, limit, slope, True), shares(count, rows * top, limit, slope, False)
    places = jnp.arange(count)

    def named(sizes, offset_by):
        used = int((sizes > 0).sum())
        fixed = max(1, used // 4)
        shifted = fixed + (places - fixed + offset_by * (used - fixed)) % max(1, count - fixed)
        return jnp.zeros((count,), jnp.int32).at[sequence[jnp.where(places < fixed, places, shifted)]].set(jnp.asarray(sizes, jnp.int32))

    sizes = jnp.where(number % 4 == 0, named(heavy_load, number // 4), named(common, number - number // 4 - 1))
    mixed = jax.random.permutation(jax.random.fold_in(own, 3), count)
    donor, sink = mixed[0:count // 2 * 2:2], mixed[1:count // 2 * 2:2]
    room = jnp.minimum(sizes[donor] - 1, limit - sizes[sink]) // 2
    room = jnp.where((donor == sequence[0]) | (sink == sequence[0]) | (sizes[sink] == 0), 0, jnp.maximum(room, 0))
    shifted = jax.random.randint(jax.random.fold_in(own, 4), (count // 2,), 0, 1 << 20) % (room + 1)
    sizes = sizes.at[donor].add(-shifted).at[sink].add(shifted)
    items = jnp.searchsorted(jnp.cumsum(sizes), jnp.arange(rows * top), side="right").astype(jnp.int32)
    grid = items.reshape(top, rows).T
    grid = grid[jax.random.permutation(jax.random.fold_in(own, 1), rows)]
    offset_by = jax.random.randint(jax.random.fold_in(own, 2), (rows, 1), 0, top)
    return jnp.take_along_axis(grid, (jnp.arange(top)[None, :] + offset_by) % top, axis=1)


def shares(count, total, bound, skew, full):
    portions = [(1 << 20) // math.isqrt(rank ** skew) + 1 for rank in range(1, count + 1)]
    largest = bound if full else min(bound, max(-(-total // count), total * portions[0] // sum(portions)))
    least = 1 if total - largest >= count - 1 else 0
    given, rest = [largest] + [least] * (count - 1), total - largest - least * (count - 1)
    while rest > 0:
        movable = [i for i in range(1, count) if given[i] < largest] or [i for i in range(1, count) if given[i] < bound]
        pool, remaining = sum([portions[i] for i in movable]), rest
        for i in movable:
            addition = min(bound - given[i], max(1, remaining * portions[i] // pool), rest)
            given[i] = given[i] + addition
            rest = rest - addition
    return np.array(given)


def bell_draw(stream_key, extent, scale, bound, split=(), held_as=jnp.bfloat16):
    gain = shard_levels(stream_key, extent, split, -0.22, 0.18) if split else 1.0
    drawn = jax.random.normal(stream_key, extent, jnp.float32) * scale * gain
    return jnp.minimum(jnp.maximum(drawn, -bound), bound).astype(held_as)


def heavy_noise(own_key, dims, scale, most, shards, heavy, held_as=jnp.bfloat16):
    values = scale * jax.random.normal(own_key, dims, jnp.float32)
    if shards:
        values = values * shard_levels(own_key, dims, shards, -0.22, 0.18)
    return jnp.clip(strengthened(values, jax.random.fold_in(own_key, 3), *heavy), -most, most).astype(held_as)


def setup_inputs(seed: int = 0) -> dict:
    splits = jax.random.split(jax.random.key(seed), 13)
    activations = bell_draw(splits[0], (N_SECTION, SECTION_TOKENS, D), 0.5, 4.0, ((0, 2), (1, 32), (2, 4)))
    queries = draw_queries(jax.random.fold_in(splits[12], 71), 0)
    keys = draw_keys(jax.random.fold_in(splits[12], 71), 0)
    values = bell_draw(splits[3], (N_SECTION, SECTION_TOKENS, KEY_VALUE_HEADS * HEAD_SIZE), 1.0, 6.0, ((0, 2), (1, 32), (2, 4)))
    segments = jax.vmap(lambda own: jnp.searchsorted(jnp.cumsum(uneven(own, DOCS, SECTION_TOKENS, SECTION_TOKENS // 2, 2)), jnp.arange(SECTION_TOKENS), side="right"))(jax.random.split(splits[4], N_SECTION)).reshape((N_SECTION, SECTION_TOKENS)).astype(jnp.int32)
    routes_keys = jax.random.split(jax.random.fold_in(splits[5], 1), N_SECTION * SECTION_TOKENS // TOK_DEV)
    routes_turns = jax.random.permutation(jax.random.fold_in(splits[5], 3), N_SECTION * SECTION_TOKENS // TOK_DEV)
    routes = jax.vmap(lambda own, number: shared_out(jax.random.fold_in(splits[5], 2), own, number, TOK_DEV, EXPERTS, TOPK, CAP, 2))(routes_keys, routes_turns).reshape((N_SECTION, SECTION_TOKENS, TOPK))
    route_weight = jnp.clip(jnp.exp(math.log(1.0) - 2.3025851 * jax.random.uniform(splits[6], (N_SECTION, SECTION_TOKENS, TOPK), jnp.float32) ** shard_levels(splits[6], (N_SECTION, SECTION_TOKENS, TOPK), ((0, 2), (1, 32)), -0.2, 0.2)), 0.1, 1.0)
    norm_gain = jnp.clip(jnp.exp(math.log(4.0) - 2.7725887 * jax.random.uniform(splits[7], (N_SECTION, D), jnp.float32) ** shard_levels(splits[7], (N_SECTION, D), ((0, 2), (1, 4)), -0.2, 0.2)), 0.25, 4.0).astype(jnp.bfloat16)
    w_out = heavy_noise(splits[8], (N_SECTION, QUERY_HEADS * HEAD_SIZE, D), (QUERY_HEADS * HEAD_SIZE) ** -0.5, 0.1875, ((0, 2), (1, 4), (2, 32)), (1, 2, 32, 2.75))
    w_gate = bell_draw(splits[9], (N_SECTION, EXPERTS, HID, D), D ** -0.5, 0.09375, ((0, 2), (1, 32), (2, 4)))
    w_up = bell_draw(splits[10], (N_SECTION, EXPERTS, HID, D), D ** -0.5, 0.09375, ((0, 2), (1, 32), (2, 4)))
    w_down = bell_draw(splits[11], (N_SECTION, EXPERTS, HID, D), HID ** -0.5, 0.21875, ((0, 2), (1, 32), (3, 4)))
    return dict(activations=activations, queries=queries, keys=keys, values=values, segments=segments, routes=routes, route_weight=route_weight, norm_gain=norm_gain, w_out=w_out, w_gate=w_gate, w_up=w_up, w_down=w_down)


NEG = -1e+30
EPS = 1e-06

def attention_core(query, keys, values, segment):
    token_rows = query.shape[0]
    query_group = QUERY_HEADS // KEY_VALUE_HEADS
    q_heads = query.reshape(token_rows, QUERY_HEADS, HEAD_SIZE).transpose(1, 0, 2)
    key_heads = keys.reshape(token_rows, KEY_VALUE_HEADS, HEAD_SIZE).transpose(1, 0, 2)
    value_heads = values.reshape(token_rows, KEY_VALUE_HEADS, HEAD_SIZE).transpose(1, 0, 2)
    place = jnp.arange(token_rows, dtype=jnp.int32)
    allowed = (place[None, :] <= place[:, None]) & (segment[None, :] == segment[:, None])
    scale = 1.0 / math.sqrt(HEAD_SIZE)

    def one_head(item):
        q_rows, index = item
        k_rows = key_heads[index // query_group]
        v_rows = value_heads[index // query_group]
        score = jnp.dot(q_rows, k_rows.T, preferred_element_type=jnp.float32) * scale
        score = jnp.where(allowed, score, NEG)
        top = lax.optimization_barrier(jnp.max(score, axis=1, keepdims=True))
        weight = jnp.where(allowed, jnp.exp(score - top), 0.0)
        total = lax.optimization_barrier(jnp.sum(weight, axis=1, keepdims=True))
        mixed = jnp.dot(weight.astype(jnp.bfloat16), v_rows, preferred_element_type=jnp.float32)
        return (mixed / total).astype(jnp.bfloat16)
    heads = lax.map(one_head, (q_heads, jnp.arange(QUERY_HEADS, dtype=jnp.int32)))
    return heads.transpose(1, 0, 2).reshape(token_rows, QUERY_HEADS * HEAD_SIZE)

def expert_layer(normed, routes, route_weight, w_gate, w_up, w_down):
    token_rows = normed.shape[0]
    blocks = token_rows // TOK_DEV
    flat = routes.reshape(blocks, TOK_DEV * TOPK)
    hits = (flat[:, :, None] == jnp.arange(EXPERTS, dtype=jnp.int32)[None, None, :]).astype(jnp.int32)
    rank = lax.optimization_barrier(jnp.sum((jnp.cumsum(hits, axis=1) - 1) * hits, axis=2))
    owner = jnp.arange(blocks, dtype=jnp.int32)[:, None]
    slots = blocks * CAP
    places = ((flat * blocks + owner) * CAP + rank).reshape(-1).astype(jnp.int32)
    buffer = jnp.zeros((EXPERTS * slots, D), jnp.bfloat16).at[places].set(jnp.repeat(normed, TOPK, axis=0))
    buffer = buffer.reshape(EXPERTS, slots, D)

    def one_expert(item):
        rows, gate_w, up_w, down_w = item
        gate = jnp.dot(rows, gate_w.T, preferred_element_type=jnp.float32)
        up = jnp.dot(rows, up_w.T, preferred_element_type=jnp.float32)
        hidden = (jax.nn.silu(gate) * up).astype(jnp.bfloat16)
        return jnp.dot(hidden, down_w, preferred_element_type=jnp.float32).astype(jnp.bfloat16)
    results = lax.map(one_expert, (buffer, w_gate, w_up, w_down)).reshape(EXPERTS * slots, D)
    picked = results[places].reshape(token_rows, TOPK, D).astype(jnp.float32)
    return lax.optimization_barrier(jnp.sum(route_weight[:, :, None] * picked, axis=1))

def reference(activations, queries, keys, values, segments, routes, route_weight, norm_gain, w_out, w_gate, w_up, w_down):
    outputs = []
    for section in range(N_SECTION):
        attended = attention_core(queries[section], keys[section], values[section], segments[section])
        mixed = jnp.dot(attended, w_out[section], preferred_element_type=jnp.float32)
        resid = (activations[section].astype(jnp.float32) + mixed).astype(jnp.bfloat16)
        resid = lax.optimization_barrier(resid)
        wide = resid.astype(jnp.float32)
        stat = lax.optimization_barrier(jnp.mean(wide * wide, axis=1, keepdims=True))
        normed = (wide * lax.rsqrt(stat + EPS) * norm_gain[section].astype(jnp.float32)[None, :]).astype(jnp.bfloat16)
        moe = expert_layer(normed, routes[section], route_weight[section], w_gate[section], w_up[section], w_down[section])
        outputs.append((wide + moe).astype(jnp.bfloat16))
    passed = jnp.stack([outputs[(section - 1) % N_SECTION] for section in range(N_SECTION)])
    passed_segments = jnp.stack([segments[(section - 1) % N_SECTION] for section in range(N_SECTION)])
    return (passed, passed_segments)
```

```python
import functools
import math

import jax
import jax.numpy as jnp
from jax import lax
from jax.experimental import pallas as pl
from jax.experimental.pallas import tpu as pltpu
from jax.sharding import PartitionSpec as P

MESH = pl.DeviceIdType.MESH
HEAD = 128
NZ = 8
FOLD = 4
NEG = -1e30
EPS = 1e-06
CAP = 20
F32 = jnp.float32
BF16 = jnp.bfloat16


def place(x, z, c):
    return x * (2 * NZ) + lax.rem(z + 2 * NZ, NZ) * 2 + c


class Net:
    def __init__(self, send, recv):
        self.send_sems, self.recv_sems = send, recv
        cp = lax.axis_index("cp")
        self.cp = cp
        self.x = cp // (2 * NZ)
        self.z = (cp // 2) % NZ
        self.c = cp % 2
        self.f = lax.axis_index("fold")
        self.xp = 1 - self.x
        self.fp, self.fo, self.fm = [lax.rem(self.f + k, FOLD) for k in (1, 2, 3)]
        self.ids = {}
        self.sent = []

    def to(self, way):
        x, z, c = self.x, self.z, self.c
        if way == "z+":
            return {"cp": place(x, z + 1, c)}
        if way == "z-":
            return {"cp": place(x, z - 1, c)}
        if way == "x":
            return {"cp": place(1 - x, z, c)}
        if way == "c":
            return {"cp": place(x, z, 1 - c)}
        if way == "f+":
            return {"fold": self.fp}
        if way == "f-":
            return {"fold": self.fm}
        if way == "fo":
            return {"fold": self.fo}
        return {"section": 1 - lax.axis_index("section")}

    def barrier(self, ways):
        sem = pltpu.get_barrier_semaphore()
        for way in ways:
            pl.semaphore_signal(sem, inc=1, device_id=self.to(way), device_id_type=MESH)
        pl.semaphore_wait(sem, len(ways))

    def slot(self, name):
        return self.ids.setdefault(name, len(self.ids))

    def copy(self, name, src, dst, way):
        i = self.slot(name)
        return pltpu.make_async_remote_copy(
            src_ref=src,
            dst_ref=dst,
            send_sem=self.send_sems.at[i],
            recv_sem=self.recv_sems.at[i],
            device_id=self.to(way),
            device_id_type=MESH,
        )

    def push(self, name, src, dst, way):
        copy = self.copy(name, src, dst, way)
        copy.start()
        self.sent.append(copy)

    def await_(self, name, dst, way):
        self.copy(name, dst, dst, way).wait_recv()

    def finish(self):
        for copy in self.sent:
            copy.wait_send()


class Gather:
    def __init__(self, net, name, buf, own, rows1):
        self.net, self.name, self.buf, self.own = net, name, buf, own
        self.rows = buf.shape[1]
        self.rows1 = rows1

    def block(self, x, z, c, part="full"):
        ref = self.buf.at[place(x, z, c)]
        if part == "full":
            return ref
        if part == "r1":
            return ref.at[pl.ds(0, self.rows1)]
        return ref.at[pl.ds(self.rows1, self.rows - self.rows1)]

    def push(self, tag, key, way, part="full", src=None):
        ref = self.block(*key, part)
        self.net.push((self.name, tag), ref if src is None else src, ref, way)

    def wait(self, tag, key, way, part="full"):
        self.net.await_((self.name, tag), self.block(*key, part), way)

    def tick(self, s):
        n = self.net
        x, z, c, xp, cp = n.x, n.z, n.c, n.xp, 1 - n.c
        if s == 0:
            for tag, way in (("zp0", "z+"), ("zm0", "z-"), ("x0", "x"), ("c0", "c")):
                self.push(tag, (x, z, c), way, src=self.own)
            return
        if s == 1:
            self.wait("x0", (xp, z, c), "x")
            self.push("yp0", (xp, z, c), "z+", "r2")
            self.push("ym0", (xp, z, c), "z-", "r2")
            self.push("cx0", (xp, z, c), "c")
        if s <= 4:
            self.wait(f"zp{s - 1}", (x, z - s, c), "z+")
            if s <= 3:
                self.push(f"zp{s}", (x, z - s, c), "z+")
                self.wait(f"zm{s - 1}", (x, z + s, c), "z-")
                if s <= 2:
                    self.push(f"zm{s}", (x, z + s, c), "z-")
            self.push(f"xm{s}", (x, z - s, c), "x", "r1")
            if s <= 3:
                self.push(f"xp{s}", (x, z + s, c), "x", "r1")
            self.push(f"cm{s}", (x, z - s, c), "c")
            if s <= 3:
                self.push(f"cp{s}", (x, z + s, c), "c")
        if s >= 2 and s <= 5:
            d = s - 1
            self.wait(f"ym{d - 1}", (xp, z + d, c), "z-", "r2")
            if d <= 3:
                self.push(f"ym{d}", (xp, z + d, c), "z-", "r2")
                self.wait(f"yp{d - 1}", (xp, z - d, c), "z+", "r2")
                if d <= 2:
                    self.push(f"yp{d}", (xp, z - d, c), "z+", "r2")
            self.push(f"dp{d}", (xp, z + d, c), "c", "r2")
            if d <= 3:
                self.push(f"dm{d}", (xp, z - d, c), "c", "r2")
            self.wait(f"xm{d}", (xp, z - d, c), "x", "r1")
            self.push(f"em{d}", (xp, z - d, c), "c", "r1")
            if d <= 3:
                self.wait(f"xp{d}", (xp, z + d, c), "x", "r1")
                self.push(f"ep{d}", (xp, z + d, c), "c", "r1")

    def ready(self, d):
        n = self.net
        x, z, xp, cp = n.x, n.z, n.xp, 1 - n.c
        if d == 0:
            self.wait("c0", (x, z, cp), "c")
            self.wait("cx0", (xp, z, cp), "c")
            return
        side, s = ("p", d) if d > 0 else ("m", -d)
        self.wait(f"c{side}{s}", (x, z + d, cp), "c")
        self.wait(f"d{'p' if s == 4 else side}{s}", (xp, z + d, cp), "c", "r2")
        self.wait(f"e{side}{s}", (xp, z + d, cp), "c", "r1")


DISTANCES = (0, -1, 1, -2, 2, -3, 3, -4)


def front(
    q, kvm, segq, act, gain, wo, wg, wu,
    resid, normed, rank, share, wg_out, wu_out,
    kvg, wog, bias, attended, hits, part, ra, rb, rc, rd, stat, send, recv, local,
):
    net = Net(send, recv)
    f, fp, fo, fm = net.f, net.fp, net.fo, net.fm
    tokens = q.shape[0]
    hid = wg.shape[1]
    feats = wg_out.shape[2]
    heads = q.shape[1] // HEAD
    net.barrier(("z+", "z-", "x", "c", "f+", "f-", "fo"))

    kv = Gather(net, "kv", kvg, kvm, kvm.shape[0] * 3 // 5)
    out = Gather(net, "wo", wog, wo, wo.shape[0] * 5 // 8)
    kv.tick(0)
    out.tick(0)
    kvg[net.cp] = kvm[...]
    keep = [pltpu.make_async_copy(wo, wog.at[net.cp], local.at[0])]
    for k, (src, dst) in enumerate(((wg, wg_out), (wu, wu_out))):
        rows = pl.ds(f * hid, hid)
        for way, t in (("f+", fp), ("f-", fm), ("fo", fo)):
            net.push(("w", k, way), src.at[:, :, pl.ds(t * feats, feats)], dst.at[:, rows, :], way)
        keep.append(
            pltpu.make_async_copy(src.at[:, :, pl.ds(f * feats, feats)], dst.at[:, rows, :], local.at[k + 1])
        )
    for copy in keep:
        copy.start()

    for s in range(1, 6):
        kv.tick(s)
        if s == 4:
            out.tick(1)
    for d in DISTANCES:
        kv.ready(d)
    out.tick(2)

    window = 17
    start = jnp.maximum(net.cp - (window - 1), 0)
    span = window * tokens
    seg_k = jnp.concatenate(
        [kvg[start + i, tokens:tokens + 16, HEAD:2 * HEAD].astype(F32)[0:1] for i in range(window)], axis=1
    )
    q_place = net.cp * tokens + lax.broadcasted_iota(jnp.int32, (tokens, span), 0)
    k_place = start * tokens + lax.broadcasted_iota(jnp.int32, (tokens, span), 1)
    allowed = (k_place <= q_place) & (seg_k == segq[:, 0:1])
    bias[...] = jnp.where(allowed, 0.0, NEG)
    factor = math.log2(math.e) / math.sqrt(HEAD)

    def head(h, carry):
        columns = pl.ds(pl.multiple_of(h * HEAD, HEAD), HEAD)
        keys = kvg[pl.ds(start, window), 0:tokens, 0:HEAD].reshape(span, HEAD)
        vals = kvg[pl.ds(start, window), 0:tokens, HEAD:2 * HEAD].reshape(span, HEAD)
        score = lax.dot_general(q[:, columns], keys, (((1,), (1,)), ((), ())), preferred_element_type=F32)
        score = score * factor + bias[...]
        top = jnp.max(score, axis=1, keepdims=True)
        weight = jnp.exp2(score - top)
        total = jnp.sum(weight, axis=1, keepdims=True)
        mixed = jnp.dot(weight.astype(BF16), vals, preferred_element_type=F32)
        attended[:, columns] = (mixed / total).astype(BF16)
        return carry

    lax.fori_loop(0, heads // 2, head, 0)
    out.tick(3)
    lax.fori_loop(heads // 2, heads, head, 0)

    for g in range(NZ):
        for e in range(2):
            expert = (2 * net.cp + e).astype(F32)
            for k in range(4):
                block = place(k // 2, g, k % 2)
                meta = kvg[block, tokens:tokens + 32, 0:tokens].astype(F32)
                chosen = meta[0:8] == expert
                row = pl.ds(2 * g + e, 1)
                columns = pl.ds(k * tokens, tokens)
                hits[row, columns] = jnp.sum(jnp.where(chosen, 1.0, 0.0), axis=0, keepdims=True)
                shares = meta[8:16] + meta[16:24] + meta[24:32]
                share[row, columns] = jnp.sum(jnp.where(chosen, shares, 0.0), axis=0, keepdims=True)
    out.tick(4)
    wide = 4 * tokens
    earlier = lax.broadcasted_iota(jnp.int32, (wide, wide), 0) < lax.broadcasted_iota(jnp.int32, (wide, wide), 1)
    hit = hits[...]
    before = jnp.dot(hit.astype(BF16), jnp.where(earlier, 1.0, 0.0).astype(BF16), preferred_element_type=F32)
    rank[...] = jnp.where(hit > 0.5, before, -1.0)
    out.tick(5)
    for d in DISTANCES:
        out.ready(d)
    keep[0].wait()

    per = 2 * NZ * 2 // FOLD
    cut = wo.shape[1]

    def project(t):
        lhs = attended[...]
        for i in range(per):
            part[t, :, i * cut:(i + 1) * cut] = jnp.dot(
                lhs, wog[t * per + i], preferred_element_type=F32
            ).astype(BF16)

    half = feats // 2
    project(fo)
    net.push("pa", part.at[fo, :, pl.ds(0, half)], ra, "f+")
    net.push("pb", part.at[fo, :, pl.ds(half, half)], rb, "f-")
    project(fp)
    project(fm)
    net.await_("pa", ra, "f+")
    part[fp, :, 0:half] = (part[fp, :, 0:half].astype(F32) + ra[...].astype(F32)).astype(BF16)
    net.push("pc", part.at[fp], rc, "f+")
    net.await_("pb", rb, "f-")
    part[fm, :, half:2 * half] = (part[fm, :, half:2 * half].astype(F32) + rb[...].astype(F32)).astype(BF16)
    net.push("pd", part.at[fm], rd, "f-")
    project(f)
    base = act[...].astype(F32) + part[f].astype(F32)
    net.await_("pc", rc, "f+")
    net.await_("pd", rd, "f-")
    kept = (base + rc[...].astype(F32) + rd[...].astype(F32)).astype(BF16)
    resid[...] = kept
    local_wide = kept.astype(F32)
    squares = jnp.sum(local_wide * local_wide, axis=1, keepdims=True)
    stat[0] = jnp.broadcast_to(squares, stat.shape[1:])
    for k, way in enumerate(("f+", "f-", "fo")):
        net.push(("s", k), stat.at[0], stat.at[k + 1], way)
    for k, way in enumerate(("f+", "f-", "fo")):
        net.await_(("s", k), stat.at[k + 1], way)
    total = (stat[0] + stat[1] + stat[2] + stat[3])[:, 0:1]
    scale = lax.rsqrt(total / (feats * FOLD) + EPS)
    normed[...] = (local_wide * scale * gain[...].astype(F32)).astype(BF16)

    for k, dst in enumerate((wg_out, wu_out)):
        for way, t in (("f+", fm), ("f-", fp), ("fo", fo)):
            net.await_(("w", k, way), dst.at[:, pl.ds(t * hid, hid), :], way)
        keep[k + 1].wait()
    net.finish()


STAGES = ((0, -1), (1, -2), (2, -3), (3, -4))


def back(
    xn, resid, rank, share, wg, wu, wd,
    passed,
    xg, wgv, wuv, wdv, slots, part, ra, rb, rc, rd, hidden, ysum, cin, xin, zin, yin, tin, result,
    send, recv, local,
):
    net = Net(send, recv)
    x, z, c, xp, cpeer = net.x, net.z, net.c, net.xp, 1 - net.c
    f, fp, fo, fm = net.f, net.fp, net.fo, net.fm
    tokens = xn.shape[0]
    hid = wgv.shape[1]
    cap = part.shape[2]
    net.barrier(("z+", "z-", "x", "c", "f+", "f-", "sec"))
    rows1 = tokens * 5 // 8
    rows2 = tokens - rows1
    xs = Gather(net, "x", xg, xn, rows1)
    xs.tick(0)
    loads = [
        pltpu.make_async_copy(src, dst, local.at[k]) for k, (src, dst) in enumerate(((wg, wgv), (wu, wuv), (wd, wdv)))
    ]
    for copy in loads:
        copy.start()
    xg[net.cp] = xn[...]

    def group(d):
        return lax.rem(z + d + NZ, NZ)

    def pick(d, e):
        row = rank[pl.ds(2 * group(d) + e, 1), :]
        want = lax.broadcasted_iota(jnp.int32, (cap, 4 * tokens), 0).astype(F32)
        return jnp.where(want == row, 1.0, 0.0)

    def enter(i):
        for j, d in enumerate(STAGES[i]):
            xs.ready(d)
            g = group(d)
            low = xg[pl.ds(2 * g, 2)].reshape(2 * tokens, xn.shape[1])
            high = xg[pl.ds(2 * NZ + 2 * g, 2)].reshape(2 * tokens, xn.shape[1])
            choice = jnp.concatenate([pick(d, 0), pick(d, 1)], axis=0).astype(BF16)
            got = jnp.dot(choice[:, 0:2 * tokens], low, preferred_element_type=F32)
            got = (got + jnp.dot(choice[:, 2 * tokens:], high, preferred_element_type=F32)).astype(BF16)
            for e in range(2):
                slots[pl.ds((2 * e + j) * cap, cap), :] = got[e * cap:(e + 1) * cap]
        for e in range(2):
            lhs = slots[pl.ds(2 * e * cap, 2 * cap), :]
            for k, w in enumerate((wgv, wuv)):
                out = lax.dot_general(lhs, w[e], (((1,), (1,)), ((), ())), preferred_element_type=F32).astype(BF16)
                part[i, 2 * e, :, k * hid:(k + 1) * hid] = out[0:cap]
                part[i, 2 * e + 1, :, k * hid:(k + 1) * hid] = out[cap:]
        net.push(("a", i), part.at[i, fo, :, pl.ds(0, hid)], ra.at[i], "f+")
        net.push(("b", i), part.at[i, fo, :, pl.ds(hid, hid)], rb.at[i], "f-")

    def relay(i):
        net.await_(("a", i), ra.at[i], "f+")
        part[i, fp, :, 0:hid] = (part[i, fp, :, 0:hid].astype(F32) + ra[i].astype(F32)).astype(BF16)
        net.push(("c", i), part.at[i, fp], rc.at[i], "f+")
        net.await_(("b", i), rb.at[i], "f-")
        part[i, fm, :, hid:2 * hid] = (part[i, fm, :, hid:2 * hid].astype(F32) + rb[i].astype(F32)).astype(BF16)
        net.push(("d", i), part.at[i, fm], rd.at[i], "f-")

    def activate(i):
        net.await_(("c", i), rc.at[i], "f+")
        net.await_(("d", i), rd.at[i], "f-")
        total = part[i, f].astype(F32) + rc[i].astype(F32) + rd[i].astype(F32)
        gate, up = total[:, 0:hid], total[:, hid:2 * hid]
        hidden[i, f] = (gate / (1.0 + jnp.exp(-gate)) * up).astype(BF16)
        net.push(("h+", i), hidden.at[i, f], hidden.at[i, f], "f+")
        net.push(("h-", i), hidden.at[i, f], hidden.at[i, f], "f-")

    def spread(i):
        half = hid // 2
        net.await_(("h+", i), hidden.at[i, fm], "f+")
        lower = hidden.at[i, fm, :, pl.ds(0, half)]
        net.push(("i+", i), lower, lower, "f+")
        net.await_(("h-", i), hidden.at[i, fp], "f-")
        upper = hidden.at[i, fp, :, pl.ds(half, half)]
        net.push(("i-", i), upper, upper, "f-")

    def leave(i):
        half = hid // 2
        net.await_(("i+", i), hidden.at[i, fo, :, pl.ds(0, half)], "f+")
        net.await_(("i-", i), hidden.at[i, fo, :, pl.ds(half, half)], "f-")
        for e in range(2):
            lhs = hidden[i, 2 * e:2 * e + 2].reshape(2 * cap, hid)
            res = jnp.dot(lhs, wdv[e], preferred_element_type=F32)
            for j, d in enumerate(STAGES[i]):
                row = share[pl.ds(2 * group(d) + e, 1), :]
                weight = jnp.sum(pick(d, e) * row, axis=1, keepdims=True)
                result[2 * j + e] = (res[j * cap:(j + 1) * cap] * weight).astype(BF16)
        for j, d in enumerate(STAGES[i]):
            g = group(d)
            choice = jnp.concatenate([pick(d, 0), pick(d, 1)], axis=0).astype(BF16)
            res = result[2 * j:2 * j + 2].reshape(2 * cap, result.shape[2])
            total = lax.dot_general(choice, res, (((0,), (0,)), ((), ())), preferred_element_type=F32).astype(BF16)
            for k in range(4):
                ysum[place(k // 2, g, k % 2)] = total[k * tokens:(k + 1) * tokens]
            for xx in range(2):
                net.push(("rc", d, xx), ysum.at[place(xx, g, cpeer)], cin.at[g, xx], "c")

    def accumulate(ref, at, rows, inc):
        ref[at, rows] = (ref[at, rows].astype(F32) + inc.astype(F32)).astype(BF16)

    def merge(i):
        for d in STAGES[i]:
            g = group(d)
            for xx in range(2):
                net.await_(("rc", d, xx), cin.at[g, xx], "c")
                accumulate(ysum, place(xx, g, c), pl.ds(0, tokens), cin[g, xx])
            net.push(("rx", d), ysum.at[place(xp, g, c), pl.ds(0, rows1)], xin.at[g], "x")

    def cross(i):
        for d in STAGES[i]:
            g = group(d)
            net.await_(("rx", d), xin.at[g], "x")
            accumulate(ysum, place(x, g, c), pl.ds(0, rows1), xin[g])

    xs.tick(1)
    xs.tick(2)
    for copy in loads:
        copy.wait()
    enter(0)
    xs.tick(3)
    enter(1)
    relay(0)
    xs.tick(4)
    enter(2)
    relay(1)
    activate(0)
    xs.tick(5)
    enter(3)
    relay(2)
    activate(1)
    spread(0)
    relay(3)
    activate(2)
    spread(1)
    leave(0)
    activate(3)
    spread(2)
    leave(1)
    merge(0)
    spread(3)
    leave(2)
    merge(1)
    cross(0)
    leave(3)
    merge(2)
    cross(1)
    merge(3)
    cross(2)
    cross(3)

    full = pl.ds(0, tokens)
    rest = pl.ds(rows1, rows2)
    lines = (("z-", -1, 4, x, zin, 0, full), ("z+", 1, 3, x, zin, 4, full), ("z-", -1, 3, xp, yin, 0, rest), ("z+", 1, 4, xp, yin, 3, rest))
    for step in range(4):
        for k, (way, sign, hops, line, inbox, first, rows) in enumerate(lines):
            s = step - (4 - hops)
            if s < 0:
                continue
            at = place(line, z + sign * (hops - s), c)
            if s > 0:
                net.await_(("rz", k, s - 1), inbox.at[first + s - 1], way)
                accumulate(ysum, at, rows, inbox[first + s - 1])
            net.push(("rz", k, s), ysum.at[at, rows], inbox.at[first + s], way)
    for k, (way, sign, hops, line, inbox, first, rows) in reversed(tuple(enumerate(lines))):
        net.await_(("rz", k, hops - 1), inbox.at[first + hops - 1], way)
        accumulate(ysum, place(line, z, c), rows, inbox[first + hops - 1])
        if k == 2:
            net.push("rt", ysum.at[place(xp, z, c), rest], tin, "x")
    net.await_("rt", tin, "x")
    moe = ysum[net.cp].astype(F32)
    own = resid[...].astype(F32) + moe
    ahead = own[0:rows1].astype(BF16)
    behind = (own[rows1:] + tin[...].astype(F32)).astype(BF16)
    xg[net.cp, 0:rows1] = ahead
    xg[net.cp, rows1:tokens] = behind
    net.push("out", xg.at[net.cp], passed, "sec")
    net.await_("out", passed, "sec")
    net.finish()


def vmem(count):
    return [pl.BlockSpec(memory_space=pltpu.VMEM)] * count


def anywhere(count):
    return [pl.BlockSpec(memory_space=pl.ANY)] * count


def sized(shape, dtype):
    return jax.ShapeDtypeStruct(shape, dtype)


def run_front(q, kvm, segq, act, gain, wo, wg, wu):
    tokens, feats = act.shape
    blocks = 4 * NZ
    span = 17 * tokens
    experts, hid, wide = wg.shape
    dma = pltpu.SemaphoreType.DMA
    return pl.pallas_call(
        front,
        out_shape=(
            sized((tokens, feats), BF16),
            sized((tokens, feats), BF16),
            sized((2 * NZ, 4 * tokens), F32),
            sized((2 * NZ, 4 * tokens), F32),
            sized((experts, hid * FOLD, wide // FOLD), BF16),
            sized((experts, hid * FOLD, wide // FOLD), BF16),
        ),
        in_specs=vmem(6) + anywhere(2),
        out_specs=tuple(vmem(4) + anywhere(2)),
        scratch_shapes=[
            pltpu.VMEM((blocks,) + kvm.shape, BF16),
            pltpu.VMEM((blocks,) + wo.shape, BF16),
            pltpu.VMEM((tokens, span), F32),
            pltpu.VMEM(q.shape, BF16),
            pltpu.VMEM((2 * NZ, 4 * tokens), F32),
            pltpu.VMEM((FOLD, tokens, feats), BF16),
            pltpu.VMEM((tokens, feats // 2), BF16),
            pltpu.VMEM((tokens, feats // 2), BF16),
            pltpu.VMEM((tokens, feats), BF16),
            pltpu.VMEM((tokens, feats), BF16),
            pltpu.VMEM((4, tokens, 128), F32),
            dma((112,)),
            dma((112,)),
            dma((3,)),
        ],
        compiler_params=pltpu.CompilerParams(collective_id=0, has_side_effects=True, vmem_limit_bytes=56 * 2**20),
        name="front",
    )(q, kvm, segq, act, gain, wo, wg, wu)


def run_back(xn, resid, rank, share, wg, wu, wd):
    tokens, feats = xn.shape
    blocks = 4 * NZ
    hid = wg.shape[1]
    cap = 4 * CAP
    rows1 = tokens * 5 // 8
    dma = pltpu.SemaphoreType.DMA
    return pl.pallas_call(
        back,
        out_shape=sized((tokens, feats), BF16),
        in_specs=vmem(4) + anywhere(3),
        out_specs=vmem(1)[0],
        scratch_shapes=[
            pltpu.VMEM((blocks, tokens, feats), BF16),
            pltpu.VMEM(wg.shape, BF16),
            pltpu.VMEM(wu.shape, BF16),
            pltpu.VMEM(wd.shape, BF16),
            pltpu.VMEM((4 * cap, feats), BF16),
            pltpu.VMEM((4, FOLD, cap, 2 * hid), BF16),
            pltpu.VMEM((4, cap, hid), BF16),
            pltpu.VMEM((4, cap, hid), BF16),
            pltpu.VMEM((4, cap, 2 * hid), BF16),
            pltpu.VMEM((4, cap, 2 * hid), BF16),
            pltpu.VMEM((4, FOLD, cap, hid), BF16),
            pltpu.VMEM((blocks, tokens, feats), BF16),
            pltpu.VMEM((NZ, 2, tokens, feats), BF16),
            pltpu.VMEM((NZ, rows1, feats), BF16),
            pltpu.VMEM((7, tokens, feats), BF16),
            pltpu.VMEM((7, tokens - rows1, feats), BF16),
            pltpu.VMEM((tokens - rows1, feats), BF16),
            pltpu.VMEM((4, cap, feats), BF16),
            dma((144,)),
            dma((144,)),
            dma((3,)),
        ],
        compiler_params=pltpu.CompilerParams(collective_id=1, has_side_effects=True, vmem_limit_bytes=60 * 2**20),
        name="back",
    )(xn, resid, rank, share, wg, wu, wd)


def body(
    activations, queries, keys, values, segments, routes, route_weight, norm_gain, w_out, w_gate, w_up, w_down,
):
    segment = segments[0]
    tokens = segment.shape[0]
    weight = route_weight[0].T
    first = lax.reduce_precision(weight, 8, 7)
    second = lax.reduce_precision(weight - first, 8, 7)
    third = weight - first - second
    meta = jnp.concatenate([routes[0].T.astype(F32), first, second, third], axis=0)
    side = jnp.broadcast_to(segment.astype(F32)[None, :], (32, tokens))
    kvm = jnp.concatenate(
        [
            jnp.concatenate([keys[0], values[0]], axis=1),
            jnp.concatenate([meta, side], axis=1).astype(BF16),
        ],
        axis=0,
    )
    segq = jnp.broadcast_to(segment.astype(F32)[:, None], (tokens, 128))
    resid, normed, rank, share, wg, wu = run_front(
        queries[0], kvm, segq, activations[0], norm_gain, w_out[0], w_gate[0], w_up[0]
    )
    passed = run_back(normed, resid, rank, share, wg, wu, w_down[0])
    moved = lax.ppermute(segments, "section", [(0, 1), (1, 0)])
    return passed[None], moved


def solution(mesh):
    return jax.shard_map(
        body,
        mesh=mesh,
        in_specs=(
            P("section", "cp", "fold"),
            P("section", "cp", "fold"),
            P("section", "cp", "fold"),
            P("section", "cp", "fold"),
            P("section", "cp"),
            P("section", "cp", None),
            P("section", "cp", None),
            P("section", "fold"),
            P("section", "fold", "cp"),
            P("section", "cp", "fold", None),
            P("section", "cp", "fold", None),
            P("section", "cp", None, "fold"),
        ),
        out_specs=(P("section", "cp", "fold"), P("section", "cp")),
        check_vma=False,
    )
```

```python
import math

import jax
import jax.numpy as jnp
from jax import lax
from jax.experimental import pallas as pl
from jax.experimental.pallas import tpu as pltpu
from jax.sharding import PartitionSpec as P

MESH = pl.DeviceIdType.MESH
HEAD = 128
NZ = 8
FOLD = 4
NEG = -1e30
EPS = 1e-06
CAP = 20
F32 = jnp.float32
BF16 = jnp.bfloat16


def place(x, z, c):
    return x * (2 * NZ) + lax.rem(z + 2 * NZ, NZ) * 2 + c


class Net:
    def __init__(self, send, recv):
        self.send_sems, self.recv_sems = send, recv
        cp = lax.axis_index("cp")
        self.cp = cp
        self.x = cp // (2 * NZ)
        self.z = (cp // 2) % NZ
        self.c = cp % 2
        self.f = lax.axis_index("fold")
        self.xp = 1 - self.x
        self.fp, self.fo, self.fm = [lax.rem(self.f + k, FOLD) for k in (1, 2, 3)]
        self.ids = {}
        self.sent = []

    def to(self, way):
        x, z, c = self.x, self.z, self.c
        if way == "z+":
            return {"cp": place(x, z + 1, c)}
        if way == "z-":
            return {"cp": place(x, z - 1, c)}
        if way == "x":
            return {"cp": place(1 - x, z, c)}
        if way == "c":
            return {"cp": place(x, z, 1 - c)}
        if way == "f+":
            return {"fold": self.fp}
        if way == "f-":
            return {"fold": self.fm}
        if way == "fo":
            return {"fold": self.fo}
        return {"section": 1 - lax.axis_index("section")}

    def greet(self, ways):
        for way in ways:
            pl.semaphore_signal(
                pltpu.get_barrier_semaphore(), inc=1, device_id=self.to(way), device_id_type=MESH
            )

    def meet(self, ways):
        pl.semaphore_wait(pltpu.get_barrier_semaphore(), len(ways))

    def slot(self, name):
        return self.ids.setdefault(name, len(self.ids))

    def copy(self, name, src, dst, way):
        i = self.slot(name)
        return pltpu.make_async_remote_copy(
            src_ref=src,
            dst_ref=dst,
            send_sem=self.send_sems.at[i],
            recv_sem=self.recv_sems.at[i],
            device_id=self.to(way),
            device_id_type=MESH,
        )

    def push(self, name, src, dst, way):
        copy = self.copy(name, src, dst, way)
        copy.start()
        self.sent.append((name[0], copy))

    def await_(self, name, dst, way):
        self.copy(name, dst, dst, way).wait_recv()

    def drain(self, *kinds):
        for kind, copy in self.sent:
            if not kinds or kind in kinds:
                copy.wait_send()
        self.sent = [entry for entry in self.sent if kinds and entry[0] not in kinds]


class Gather:
    def __init__(self, net, name, buf, rows1):
        self.net, self.name, self.buf = net, name, buf
        self.rows = buf.shape[1]
        self.rows1 = rows1

    def block(self, x, z, c, part="full"):
        ref = self.buf.at[place(x, z, c)]
        if part == "full":
            return ref
        if part == "r1":
            return ref.at[pl.ds(0, self.rows1)]
        return ref.at[pl.ds(self.rows1, self.rows - self.rows1)]

    def push(self, tag, key, way, part="full"):
        ref = self.block(*key, part)
        self.net.push((self.name, tag), ref, ref, way)

    def wait(self, tag, key, way, part="full"):
        self.net.await_((self.name, tag), self.block(*key, part), way)

    def tick(self, s):
        n = self.net
        x, z, c, xp, cp = n.x, n.z, n.c, n.xp, 1 - n.c
        if s == 0:
            for tag, way in (("zp0", "z+"), ("zm0", "z-"), ("x0", "x"), ("c0", "c")):
                self.push(tag, (x, z, c), way)
            return
        if s == 1:
            self.wait("x0", (xp, z, c), "x")
            self.push("yp0", (xp, z, c), "z+", "r2")
            self.push("ym0", (xp, z, c), "z-", "r2")
            self.push("cx0", (xp, z, c), "c")
        if s <= 4:
            self.wait(f"zp{s - 1}", (x, z - s, c), "z+")
            if s <= 3:
                self.push(f"zp{s}", (x, z - s, c), "z+")
                self.wait(f"zm{s - 1}", (x, z + s, c), "z-")
                if s <= 2:
                    self.push(f"zm{s}", (x, z + s, c), "z-")
            self.push(f"xm{s}", (x, z - s, c), "x", "r1")
            if s <= 3:
                self.push(f"xp{s}", (x, z + s, c), "x", "r1")
            self.push(f"cm{s}", (x, z - s, c), "c")
            if s <= 3:
                self.push(f"cp{s}", (x, z + s, c), "c")
        if s >= 2 and s <= 5:
            d = s - 1
            self.wait(f"ym{d - 1}", (xp, z + d, c), "z-", "r2")
            if d <= 3:
                self.push(f"ym{d}", (xp, z + d, c), "z-", "r2")
                self.wait(f"yp{d - 1}", (xp, z - d, c), "z+", "r2")
                if d <= 2:
                    self.push(f"yp{d}", (xp, z - d, c), "z+", "r2")
            self.push(f"dp{d}", (xp, z + d, c), "c", "r2")
            if d <= 3:
                self.push(f"dm{d}", (xp, z - d, c), "c", "r2")
            self.wait(f"xm{d}", (xp, z - d, c), "x", "r1")
            self.push(f"em{d}", (xp, z - d, c), "c", "r1")
            if d <= 3:
                self.wait(f"xp{d}", (xp, z + d, c), "x", "r1")
                self.push(f"ep{d}", (xp, z + d, c), "c", "r1")

    def ready(self, d):
        n = self.net
        x, z, xp, cp = n.x, n.z, n.xp, 1 - n.c
        if d == 0:
            self.wait("c0", (x, z, cp), "c")
            self.wait("cx0", (xp, z, cp), "c")
            return
        side, s = ("p", d) if d > 0 else ("m", -d)
        self.wait(f"c{side}{s}", (x, z + d, cp), "c")
        self.wait(f"d{'p' if s == 4 else side}{s}", (xp, z + d, cp), "c", "r2")
        self.wait(f"e{side}{s}", (xp, z + d, cp), "c", "r1")


DISTANCES = (0, -1, 1, -2, 2, -3, 3, -4)
STAGES = ((3, -4), (2, -3), (1, -2), (-1, 0))
WAYS = ("z+", "z-", "x", "c", "f+", "f-", "fo", "sec")
NT = (((1,), (1,)), ((), ()))


def layer(
    q, keys, values, segments, routes, weights, act, gain, wo, wg, wu, wd,
    passed, passed_segments,
    kvg, pool, xg, wgv, wuv, wdv, bias, attended, hits, rank, share, proj, pa, pb, pc, pd, stat,
    slots, part, ra, rb, rc, rd, hidden, result, cin, xin, zin, yin, tin, resid, done,
    send, recv, local,
):
    net = Net(send, recv)
    x, z, c, xp, cpeer = net.x, net.z, net.c, net.xp, 1 - net.c
    f, fp, fo, fm = net.f, net.fp, net.fo, net.fm
    tokens, feats = act.shape
    cap = 4 * CAP
    rows1 = tokens * 5 // 8
    rows2 = tokens - rows1
    net.greet(WAYS)

    kvg[net.cp, 0:tokens, 0:HEAD] = keys[...]
    kvg[net.cp, 0:tokens, HEAD:2 * HEAD] = values[...]
    weight = weights[...]
    first = weight.astype(BF16).astype(F32)
    second = (weight - first).astype(BF16).astype(F32)
    third = weight - first - second
    meta = jnp.concatenate([routes[...].astype(F32), first, second, third], axis=0)
    kvg[net.cp, tokens:tokens + 32, 0:HEAD] = meta.astype(BF16)
    side = jnp.broadcast_to(segments[...].astype(F32), (32, tokens)).astype(BF16)
    kvg[net.cp, tokens:tokens + 32, HEAD:2 * HEAD] = side
    eye = (
        lax.broadcasted_iota(jnp.int32, (tokens, tokens), 0) == lax.broadcasted_iota(jnp.int32, (tokens, tokens), 1)
    ).astype(F32).astype(BF16)
    seg_q = lax.dot_general(eye, side, NT, preferred_element_type=F32)[:, 0:1]
    pool[net.cp] = lax.dot_general(eye, wo[...], NT, preferred_element_type=F32).astype(BF16)

    net.meet(WAYS)
    kv = Gather(net, "kv", kvg, kvg.shape[1] * 3 // 5)
    out = Gather(net, "wo", pool, rows1)
    kv.tick(0)
    out.tick(0)
    hid = wg.shape[1]
    loads = [pltpu.make_async_copy(wd, wdv, local.at[2])]
    for k, (src, dst) in enumerate(((wg, wgv), (wu, wuv))):
        rows = pl.ds(f * hid, hid)
        for way, t in (("f+", fp), ("f-", fm), ("fo", fo)):
            net.push(("w", k, way), src.at[:, :, pl.ds(t * feats, feats)], dst.at[:, rows, :], way)
        loads.append(
            pltpu.make_async_copy(src.at[:, :, pl.ds(f * feats, feats)], dst.at[:, rows, :], local.at[k])
        )
    for copy in loads:
        copy.start()
    net.push(("seg",), segments, passed_segments, "sec")

    for s in range(1, 6):
        kv.tick(s)
        if s == 4:
            out.tick(1)
    for d in DISTANCES:
        kv.ready(d)
    out.tick(2)

    window = 17
    start = jnp.maximum(net.cp - (window - 1), 0)
    span = window * tokens
    seg_k = jnp.concatenate(
        [kvg[start + i, tokens:tokens + 16, HEAD:2 * HEAD].astype(F32)[0:1] for i in range(window)], axis=1
    )
    q_place = net.cp * tokens + lax.broadcasted_iota(jnp.int32, (tokens, span), 0)
    k_place = start * tokens + lax.broadcasted_iota(jnp.int32, (tokens, span), 1)
    allowed = (k_place <= q_place) & (seg_k == seg_q)
    bias[...] = jnp.where(allowed, 0.0, NEG)
    factor = math.log2(math.e) / math.sqrt(HEAD)

    def head(h, carry):
        columns = pl.ds(pl.multiple_of(h * HEAD, HEAD), HEAD)
        ks = kvg[pl.ds(start, window), 0:tokens, 0:HEAD].reshape(span, HEAD)
        vs = kvg[pl.ds(start, window), 0:tokens, HEAD:2 * HEAD].reshape(span, HEAD)
        score = lax.dot_general(q[:, columns], ks, NT, preferred_element_type=F32)
        score = score * factor + bias[...]
        top = jnp.max(score, axis=1, keepdims=True)
        terms = jnp.exp2(score - top)
        total = jnp.sum(terms, axis=1, keepdims=True)
        mixed = jnp.dot(terms.astype(BF16), vs, preferred_element_type=F32)
        attended[:, columns] = (mixed / total).astype(BF16)
        return carry

    heads = q.shape[1] // HEAD
    lax.fori_loop(0, heads // 2, head, 0)
    out.tick(3)
    lax.fori_loop(heads // 2, heads, head, 0)
    out.tick(4)
    out.tick(5)
    for d in DISTANCES:
        out.ready(d)

    per = 4 * NZ // FOLD

    def project(t):
        lhs = attended[...]
        for i in range(0, per, 2):
            rhs = pool[pl.ds(t * per + i, 2)].reshape(2 * tokens, lhs.shape[1])
            proj[t, :, i * tokens:(i + 2) * tokens] = lax.dot_general(
                lhs, rhs, NT, preferred_element_type=F32
            ).astype(BF16)

    half = feats // 2
    project(fo)
    net.push(("pa",), proj.at[fo, :, pl.ds(0, half)], pa, "f+")
    net.push(("pb",), proj.at[fo, :, pl.ds(half, half)], pb, "f-")
    project(fp)
    project(fm)
    net.await_(("pa",), pa, "f+")
    proj[fp, :, 0:half] = (proj[fp, :, 0:half].astype(F32) + pa[...].astype(F32)).astype(BF16)
    net.push(("pc",), proj.at[fp], pc, "f+")
    net.await_(("pb",), pb, "f-")
    proj[fm, :, half:2 * half] = (proj[fm, :, half:2 * half].astype(F32) + pb[...].astype(F32)).astype(BF16)
    net.push(("pd",), proj.at[fm], pd, "f-")
    project(f)
    base = act[...].astype(F32) + proj[f].astype(F32)
    net.await_(("pc",), pc, "f+")
    net.await_(("pd",), pd, "f-")
    kept = (base + pc[...].astype(F32) + pd[...].astype(F32)).astype(BF16)
    resid[...] = kept
    wide = kept.astype(F32)
    stat[0] = jnp.broadcast_to(jnp.sum(wide * wide, axis=1, keepdims=True), stat.shape[1:])
    for k, way in enumerate(("f+", "f-", "fo")):
        net.push(("s", k), stat.at[0], stat.at[k + 1], way)
    for k, way in enumerate(("f+", "f-", "fo")):
        net.await_(("s", k), stat.at[k + 1], way)
    total = (stat[0] + stat[1] + stat[2] + stat[3])[:, 0:1]
    scale = lax.rsqrt(total / (feats * FOLD) + EPS)
    xg[net.cp] = (wide * scale * gain[...].astype(F32)).astype(BF16)

    xs = Gather(net, "x", xg, rows1)
    xs.tick(0)

    for g in range(NZ):
        for e in range(2):
            expert = (2 * net.cp + e).astype(F32)
            for k in range(4):
                meta = kvg[place(k // 2, g, k % 2), tokens:tokens + 32, 0:tokens].astype(F32)
                chosen = meta[0:8] == expert
                row = pl.ds(2 * g + e, 1)
                columns = pl.ds(k * tokens, tokens)
                hits[row, columns] = jnp.sum(jnp.where(chosen, 1.0, 0.0), axis=0, keepdims=True)
                shares = meta[8:16] + meta[16:24] + meta[24:32]
                share[row, columns] = jnp.sum(jnp.where(chosen, shares, 0.0), axis=0, keepdims=True)
    xs.tick(1)
    wide4 = 4 * tokens
    earlier = lax.broadcasted_iota(jnp.int32, (wide4, wide4), 0) < lax.broadcasted_iota(jnp.int32, (wide4, wide4), 1)
    hit = hits[...]
    before = jnp.dot(hit.astype(BF16), jnp.where(earlier, 1.0, 0.0).astype(BF16), preferred_element_type=F32)
    rank[...] = jnp.where(hit > 0.5, before, -1.0)

    def group(d):
        return lax.rem(z + d + NZ, NZ)

    def pick(d, e):
        row = rank[pl.ds(2 * group(d) + e, 1), :]
        want = lax.broadcasted_iota(jnp.int32, (cap, 4 * tokens), 0).astype(F32)
        return jnp.where(want == row, 1.0, 0.0)

    def select(i):
        for j, d in enumerate(STAGES[i]):
            xs.ready(d)
            g = group(d)
            low = xg[pl.ds(2 * g, 2)].reshape(2 * tokens, feats)
            high = xg[pl.ds(2 * NZ + 2 * g, 2)].reshape(2 * tokens, feats)
            choice = jnp.concatenate([pick(d, 0), pick(d, 1)], axis=0).astype(BF16)
            got = jnp.dot(choice[:, 0:2 * tokens], low, preferred_element_type=F32)
            got = (got + jnp.dot(choice[:, 2 * tokens:], high, preferred_element_type=F32)).astype(BF16)
            for e in range(2):
                slots[i, pl.ds((2 * e + j) * cap, cap), :] = got[e * cap:(e + 1) * cap]

    wide_hid = FOLD * hid

    def enter(i):
        for e in range(2):
            lhs = slots[i, pl.ds(2 * e * cap, 2 * cap), :]
            for k, w in enumerate((wgv, wuv)):
                res = lax.dot_general(lhs, w[e], NT, preferred_element_type=F32).astype(BF16)
                part[i, 2 * e, :, k * wide_hid:(k + 1) * wide_hid] = res[0:cap]
                part[i, 2 * e + 1, :, k * wide_hid:(k + 1) * wide_hid] = res[cap:]
        net.push(("a", i), part.at[i, fo, :, pl.ds(0, wide_hid)], ra.at[i], "f+")
        net.push(("b", i), part.at[i, fo, :, pl.ds(wide_hid, wide_hid)], rb.at[i], "f-")

    def relay(i):
        left, right = pl.ds(0, wide_hid), pl.ds(wide_hid, wide_hid)
        net.await_(("a", i), ra.at[i], "f+")
        part[i, fp, :, left] = (part[i, fp, :, left].astype(F32) + ra[i].astype(F32)).astype(BF16)
        net.push(("c", i), part.at[i, fp], rc.at[i], "f+")
        net.await_(("b", i), rb.at[i], "f-")
        part[i, fm, :, right] = (part[i, fm, :, right].astype(F32) + rb[i].astype(F32)).astype(BF16)
        net.push(("d", i), part.at[i, fm], rd.at[i], "f-")

    def activate(i):
        net.await_(("c", i), rc.at[i], "f+")
        net.await_(("d", i), rd.at[i], "f-")
        total = part[i, f].astype(F32) + rc[i].astype(F32) + rd[i].astype(F32)
        gate, up = total[:, 0:wide_hid], total[:, wide_hid:2 * wide_hid]
        hidden[i, f] = (gate / (1.0 + jnp.exp(-gate)) * up).astype(BF16)
        net.push(("h+", i), hidden.at[i, f], hidden.at[i, f], "f+")
        net.push(("h-", i), hidden.at[i, f], hidden.at[i, f], "f-")

    half_hid = wide_hid // 2

    def spread(i):
        net.await_(("h+", i), hidden.at[i, fm], "f+")
        lower = hidden.at[i, fm, :, pl.ds(0, half_hid)]
        net.push(("i+", i), lower, lower, "f+")
        net.await_(("h-", i), hidden.at[i, fp], "f-")
        upper = hidden.at[i, fp, :, pl.ds(half_hid, half_hid)]
        net.push(("i-", i), upper, upper, "f-")

    def leave(i):
        net.await_(("i+", i), hidden.at[i, fo, :, pl.ds(0, half_hid)], "f+")
        net.await_(("i-", i), hidden.at[i, fo, :, pl.ds(half_hid, half_hid)], "f-")
        for e in range(2):
            lhs = hidden[i, 2 * e:2 * e + 2].reshape(2 * cap, wide_hid)
            res = jnp.dot(lhs, wdv[e], preferred_element_type=F32)
            for j, d in enumerate(STAGES[i]):
                row = share[pl.ds(2 * group(d) + e, 1), :]
                scaled = jnp.sum(pick(d, e) * row, axis=1, keepdims=True)
                result[2 * j + e] = (res[j * cap:(j + 1) * cap] * scaled).astype(BF16)
        for j, d in enumerate(STAGES[i]):
            g = group(d)
            choice = jnp.concatenate([pick(d, 0), pick(d, 1)], axis=0).astype(BF16)
            res = result[2 * j:2 * j + 2].reshape(2 * cap, feats)
            total = lax.dot_general(choice, res, (((0,), (0,)), ((), ())), preferred_element_type=F32).astype(BF16)
            for k in range(4):
                pool[place(k // 2, g, k % 2)] = total[k * tokens:(k + 1) * tokens]
            for xx in range(2):
                net.push(("rc", d, xx), pool.at[place(xx, g, cpeer)], cin.at[g, xx], "c")

    def accumulate(at, rows, inc):
        pool[at, rows] = (pool[at, rows].astype(F32) + inc.astype(F32)).astype(BF16)

    full, ahead, rest = pl.ds(0, tokens), pl.ds(0, rows1), pl.ds(rows1, rows2)

    def merge(i):
        for d in STAGES[i]:
            g = group(d)
            for xx in range(2):
                net.await_(("rc", d, xx), cin.at[g, xx], "c")
                accumulate(place(xx, g, c), full, cin[g, xx])
            net.push(("rx", d), pool.at[place(xp, g, c), ahead], xin.at[g], "x")

    def cross(d):
        g = group(d)
        net.await_(("rx", d), xin.at[g], "x")
        accumulate(place(x, g, c), ahead, xin[g])

    lines = (
        ("z-", -1, 4, x, zin, 0, full),
        ("z+", 1, 3, x, zin, 4, full),
        ("z-", -1, 3, xp, yin, 0, rest),
        ("z+", 1, 4, xp, yin, 3, rest),
    )

    def hop(k, d):
        way, sign, hops, line, inbox, first, rows = lines[k]
        s = hops - abs(d)
        at = place(line, z + d, c)
        if s > 0:
            net.await_(("rz", k, s - 1), inbox.at[first + s - 1], way)
            accumulate(at, rows, inbox[first + s - 1])
        if s < hops:
            net.push(("rz", k, s), pool.at[at, rows], inbox.at[first + s], way)

    xs.tick(2)
    xs.tick(3)
    select(3)
    xs.tick(4)
    select(2)
    xs.tick(5)
    select(1)
    select(0)
    net.drain("wo")
    for k, dst in enumerate((wgv, wuv)):
        for way, t in (("f+", fm), ("f-", fp), ("fo", fo)):
            net.await_(("w", k, way), dst.at[:, pl.ds(t * hid, hid), :], way)
    for copy in loads:
        copy.wait()

    enter(0)
    enter(1)
    relay(0)
    relay(1)
    activate(0)
    enter(2)
    activate(1)
    spread(0)
    relay(2)
    leave(0)
    spread(1)
    enter(3)
    activate(2)
    merge(0)
    leave(1)
    relay(3)
    spread(2)
    cross(-4)
    hop(0, -4)
    hop(3, 4)
    cross(3)
    hop(1, 3)
    merge(1)
    activate(3)
    leave(2)
    cross(-3)
    hop(0, -3)
    hop(2, -3)
    hop(3, 3)
    cross(2)
    spread(3)
    hop(1, 2)
    merge(2)
    hop(3, 2)
    leave(3)
    cross(1)
    hop(1, 1)
    hop(3, 1)
    cross(-2)
    hop(0, -2)
    hop(2, -2)
    merge(3)
    cross(-1)
    hop(0, -1)
    hop(2, -1)
    cross(0)
    hop(3, 0)
    hop(1, 0)
    hop(2, 0)
    net.push(("rt",), pool.at[place(xp, z, c), rest], tin, "x")
    hop(0, 0)
    own = resid[...].astype(F32) + pool[net.cp].astype(F32)
    net.await_(("rt",), tin, "x")
    done[0:rows1] = own[0:rows1].astype(BF16)
    done[rows1:tokens] = (own[rows1:] + tin[...].astype(F32)).astype(BF16)
    net.push(("out",), done, passed, "sec")
    net.await_(("seg",), passed_segments, "sec")
    net.await_(("out",), passed, "sec")
    net.drain()


def run_layer(q, keys, values, segments, routes, weights, act, gain, wo, wg, wu, wd):
    tokens, feats = act.shape
    blocks = 4 * NZ
    experts, quarter, wide = wg.shape
    hid = quarter * FOLD
    cap = 4 * CAP
    rows1 = tokens * 5 // 8
    dma = pltpu.SemaphoreType.DMA

    def scratch(*shape, dtype=BF16):
        return pltpu.VMEM(shape, dtype)

    vmem, hbm = pl.BlockSpec(memory_space=pltpu.VMEM), pl.BlockSpec(memory_space=pl.ANY)
    return pl.pallas_call(
        layer,
        out_shape=(jax.ShapeDtypeStruct((tokens, feats), BF16), jax.ShapeDtypeStruct(segments.shape, segments.dtype)),
        in_specs=[vmem] * 9 + [hbm] * 3,
        out_specs=(vmem, vmem),
        scratch_shapes=[
            scratch(blocks, tokens + 32, 2 * HEAD),
            scratch(blocks, tokens, feats),
            scratch(blocks, tokens, feats),
            scratch(experts, hid, feats),
            scratch(experts, hid, feats),
            scratch(experts, hid, feats),
            scratch(tokens, 17 * tokens, dtype=F32),
            scratch(*q.shape),
            scratch(2 * NZ, 4 * tokens, dtype=F32),
            scratch(2 * NZ, 4 * tokens, dtype=F32),
            scratch(2 * NZ, 4 * tokens, dtype=F32),
            scratch(FOLD, tokens, feats),
            scratch(tokens, feats // 2),
            scratch(tokens, feats // 2),
            scratch(tokens, feats),
            scratch(tokens, feats),
            scratch(4, tokens, 128, dtype=F32),
            scratch(4, 4 * cap, feats),
            scratch(4, FOLD, cap, 2 * hid),
            scratch(4, cap, hid),
            scratch(4, cap, hid),
            scratch(4, cap, 2 * hid),
            scratch(4, cap, 2 * hid),
            scratch(4, FOLD, cap, hid),
            scratch(4, cap, feats),
            scratch(NZ, 2, tokens, feats),
            scratch(NZ, rows1, feats),
            scratch(7, tokens, feats),
            scratch(7, tokens - rows1, feats),
            scratch(tokens - rows1, feats),
            scratch(tokens, feats),
            scratch(tokens, feats),
            dma((224,)),
            dma((224,)),
            dma((3,)),
        ],
        compiler_params=pltpu.CompilerParams(collective_id=0, has_side_effects=True, vmem_limit_bytes=62 * 2**20),
        name="layer",
    )(q, keys, values, segments, routes, weights, act, gain, wo, wg, wu, wd)


def body(
    activations, queries, keys, values, segments, routes, route_weight, norm_gain, w_out, w_gate, w_up, w_down,
):
    passed, moved = run_layer(
        queries[0], keys[0], values[0], segments, routes[0].T, route_weight[0].T, activations[0], norm_gain,
        w_out[0], w_gate[0], w_up[0], w_down[0],
    )
    return passed[None], moved


def solution(mesh):
    return jax.shard_map(
        body,
        mesh=mesh,
        in_specs=(
            P("section", "cp", "fold"),
            P("section", "cp", "fold"),
            P("section", "cp", "fold"),
            P("section", "cp", "fold"),
            P("section", "cp"),
            P("section", "cp", None),
            P("section", "cp", None),
            P("section", "fold"),
            P("section", "fold", "cp"),
            P("section", "cp", "fold", None),
            P("section", "cp", "fold", None),
            P("section", "cp", None, "fold"),
        ),
        out_specs=(P("section", "cp", "fold"), P("section", "cp")),
        check_vma=False,
    )
```

```python
import math

import jax
import jax.numpy as jnp
from jax import lax
from jax.experimental import pallas as pl
from jax.experimental.pallas import tpu as pltpu
from jax.sharding import PartitionSpec as P

MESH = pl.DeviceIdType.MESH
HEAD = 128
NZ = 8
FOLD = 4
NEG = -1e30
EPS = 1e-06
CAP = 20
F32 = jnp.float32
BF16 = jnp.bfloat16


def place(x, z, c):
    return x * (2 * NZ) + lax.rem(z + 2 * NZ, NZ) * 2 + c


class Net:
    def __init__(self, send, recv):
        self.send_sems, self.recv_sems = send, recv
        cp = lax.axis_index("cp")
        self.cp = cp
        self.x = cp // (2 * NZ)
        self.z = (cp // 2) % NZ
        self.c = cp % 2
        self.f = lax.axis_index("fold")
        self.xp = 1 - self.x
        self.fp, self.fo, self.fm = [lax.rem(self.f + k, FOLD) for k in (1, 2, 3)]
        self.ids = {}
        self.sent = []

    def to(self, way):
        x, z, c = self.x, self.z, self.c
        if way == "z+":
            return {"cp": place(x, z + 1, c)}
        if way == "z-":
            return {"cp": place(x, z - 1, c)}
        if way == "x":
            return {"cp": place(1 - x, z, c)}
        if way == "c":
            return {"cp": place(x, z, 1 - c)}
        if way == "f+":
            return {"fold": self.fp}
        if way == "f-":
            return {"fold": self.fm}
        if way == "fo":
            return {"fold": self.fo}
        return {"section": 1 - lax.axis_index("section")}

    def greet(self, ways):
        for way in ways:
            pl.semaphore_signal(
                pltpu.get_barrier_semaphore(), inc=1, device_id=self.to(way), device_id_type=MESH
            )

    def meet(self, ways):
        pl.semaphore_wait(pltpu.get_barrier_semaphore(), len(ways))

    def slot(self, name):
        return self.ids.setdefault(name, len(self.ids))

    def copy(self, name, src, dst, way):
        i = self.slot(name)
        return pltpu.make_async_remote_copy(
            src_ref=src,
            dst_ref=dst,
            send_sem=self.send_sems.at[i],
            recv_sem=self.recv_sems.at[i],
            device_id=self.to(way),
            device_id_type=MESH,
        )

    def push(self, name, src, dst, way):
        copy = self.copy(name, src, dst, way)
        copy.start()
        self.sent.append((name[0], copy))

    def await_(self, name, dst, way):
        self.copy(name, dst, dst, way).wait_recv()

    def drain(self, *kinds):
        for kind, copy in self.sent:
            if not kinds or kind in kinds:
                copy.wait_send()
        self.sent = [entry for entry in self.sent if kinds and entry[0] not in kinds]


class Gather:
    def __init__(self, net, name, buf, rows1):
        self.net, self.name, self.buf = net, name, buf
        self.rows = buf.shape[1]
        self.rows1 = rows1

    def block(self, x, z, c, part="full"):
        ref = self.buf.at[place(x, z, c)]
        if part == "full":
            return ref
        if part == "r1":
            return ref.at[pl.ds(0, self.rows1)]
        return ref.at[pl.ds(self.rows1, self.rows - self.rows1)]

    def push(self, tag, key, way, part="full"):
        ref = self.block(*key, part)
        self.net.push((self.name, tag), ref, ref, way)

    def wait(self, tag, key, way, part="full"):
        self.net.await_((self.name, tag), self.block(*key, part), way)

    def tick(self, s):
        n = self.net
        x, z, c, xp, cp = n.x, n.z, n.c, n.xp, 1 - n.c
        if s == 0:
            for tag, way in (("zp0", "z+"), ("zm0", "z-"), ("x0", "x"), ("c0", "c")):
                self.push(tag, (x, z, c), way)
            return
        if s == 1:
            self.wait("x0", (xp, z, c), "x")
            self.push("yp0", (xp, z, c), "z+", "r2")
            self.push("ym0", (xp, z, c), "z-", "r2")
            self.push("cx0", (xp, z, c), "c")
        if s <= 4:
            self.wait(f"zp{s - 1}", (x, z - s, c), "z+")
            if s <= 3:
                self.push(f"zp{s}", (x, z - s, c), "z+")
                self.wait(f"zm{s - 1}", (x, z + s, c), "z-")
                if s <= 2:
                    self.push(f"zm{s}", (x, z + s, c), "z-")
            self.push(f"xm{s}", (x, z - s, c), "x", "r1")
            if s <= 3:
                self.push(f"xp{s}", (x, z + s, c), "x", "r1")
            self.push(f"cm{s}", (x, z - s, c), "c")
            if s <= 3:
                self.push(f"cp{s}", (x, z + s, c), "c")
        if s >= 2 and s <= 5:
            d = s - 1
            self.wait(f"ym{d - 1}", (xp, z + d, c), "z-", "r2")
            if d <= 3:
                self.push(f"ym{d}", (xp, z + d, c), "z-", "r2")
                self.wait(f"yp{d - 1}", (xp, z - d, c), "z+", "r2")
                if d <= 2:
                    self.push(f"yp{d}", (xp, z - d, c), "z+", "r2")
            self.push(f"dp{d}", (xp, z + d, c), "c", "r2")
            if d <= 3:
                self.push(f"dm{d}", (xp, z - d, c), "c", "r2")
            self.wait(f"xm{d}", (xp, z - d, c), "x", "r1")
            self.push(f"em{d}", (xp, z - d, c), "c", "r1")
            if d <= 3:
                self.wait(f"xp{d}", (xp, z + d, c), "x", "r1")
                self.push(f"ep{d}", (xp, z + d, c), "c", "r1")

    def ready(self, d):
        n = self.net
        x, z, xp, cp = n.x, n.z, n.xp, 1 - n.c
        if d == 0:
            self.wait("c0", (x, z, cp), "c")
            self.wait("cx0", (xp, z, cp), "c")
            return
        side, s = ("p", d) if d > 0 else ("m", -d)
        self.wait(f"c{side}{s}", (x, z + d, cp), "c")
        self.wait(f"d{'p' if s == 4 else side}{s}", (xp, z + d, cp), "c", "r2")
        self.wait(f"e{side}{s}", (xp, z + d, cp), "c", "r1")


DISTANCES = (0, -1, 1, -2, 2, -3, 3, -4)
STAGES = ((3, -4), (2, -3), (1, -2), (-1, 0))
WAYS = ("z+", "z-", "x", "c", "f+", "f-", "fo", "sec")
NT = (((1,), (1,)), ((), ()))


def layer(
    q, keys, values, segments, routes, weights, act, gain, wo, wg, wu, wd,
    passed, passed_segments,
    kvg, pool, xg, wgv, wuv, wdv, qs, top, total, mixed, attended, hits, rank, share, proj, inbox, stat,
    slots, part, ra, rb, rc, rd, hidden, result, cin, xin, zin, yin, tin, resid, done,
    send, recv, local,
):
    net = Net(send, recv)
    x, z, c, xp, cpeer = net.x, net.z, net.c, net.xp, 1 - net.c
    f, fp, fo, fm = net.f, net.fp, net.fo, net.fm
    tokens, feats = act.shape
    cap = 4 * CAP
    rows1 = tokens * 5 // 8
    rows2 = tokens - rows1
    net.greet(WAYS)

    kvg[net.cp, 0:tokens, 0:HEAD] = keys[...]
    kvg[net.cp, 0:tokens, HEAD:2 * HEAD] = values[...]
    weight = weights[...]
    coarse = weight.astype(BF16).astype(F32)
    side = jnp.broadcast_to(segments[...].astype(F32), (8, tokens))
    meta = jnp.concatenate([routes[...].astype(F32), coarse], axis=0)
    kvg[net.cp, tokens:tokens + 16, 0:HEAD] = meta.astype(BF16)
    meta = jnp.concatenate([weight - coarse, side], axis=0)
    kvg[net.cp, tokens:tokens + 16, HEAD:2 * HEAD] = meta.astype(BF16)
    eye = (
        lax.broadcasted_iota(jnp.int32, (tokens, tokens), 0) == lax.broadcasted_iota(jnp.int32, (tokens, tokens), 1)
    ).astype(F32).astype(BF16)
    seg_q = lax.dot_general(eye, jnp.concatenate([side, side], axis=0).astype(BF16), NT, preferred_element_type=F32)[:, 0:1]
    pool[net.cp] = lax.dot_general(eye, wo[...], NT, preferred_element_type=F32).astype(BF16)

    net.meet(WAYS)
    kv = Gather(net, "kv", kvg, rows1)
    out = Gather(net, "wo", pool, rows1)
    kv.tick(0)
    out.tick(0)
    hid = wg.shape[1]
    loads = [pltpu.make_async_copy(wd, wdv, local.at[2])]
    for k, (src, dst) in enumerate(((wg, wgv), (wu, wuv))):
        rows = pl.ds(f * hid, hid)
        loads.append(
            pltpu.make_async_copy(src.at[:, :, pl.ds(f * feats, feats)], dst.at[:, rows, :], local.at[k])
        )
    for copy in loads:
        copy.start()

    def resplit(k, src, dst):
        for way, t in (("f+", fp), ("f-", fm), ("fo", fo)):
            net.push(("w", k, way), src.at[:, :, pl.ds(t * feats, feats)], dst.at[:, pl.ds(f * hid, hid), :], way)

    resplit(0, wg, wgv)
    net.push(("seg",), segments, passed_segments, "sec")

    heads = q.shape[1] // HEAD
    for h in range(heads):
        qs[h] = q[:, h * HEAD:(h + 1) * HEAD]
    top[...] = jnp.full(top.shape, NEG, F32)
    total[...] = jnp.zeros(total.shape, F32)
    mixed[...] = jnp.zeros(mixed.shape, F32)
    factor = math.log2(math.e) / math.sqrt(HEAD)
    q_place = net.cp * tokens + lax.broadcasted_iota(jnp.int32, (tokens, 2 * tokens), 0)

    def attend(line, d):
        base = place(line, z + d, 0)
        ks = kvg[pl.ds(base, 2), 0:tokens, 0:HEAD].reshape(2 * tokens, HEAD)
        vs = kvg[pl.ds(base, 2), 0:tokens, HEAD:2 * HEAD].reshape(2 * tokens, HEAD)
        seg_k = jnp.concatenate(
            [kvg[base + i, tokens:tokens + 16, HEAD:2 * HEAD].astype(F32)[8:9] for i in range(2)], axis=1
        )
        k_place = base * tokens + lax.broadcasted_iota(jnp.int32, (tokens, 2 * tokens), 1)
        bias = jnp.where((k_place <= q_place) & (seg_k == seg_q), 0.0, NEG)
        score = lax.dot_general(qs[...].reshape(heads * tokens, HEAD), ks, NT, preferred_element_type=F32)
        score = score.reshape(heads, tokens, 2 * tokens) * factor + bias[None]
        old = top[...]
        new = jnp.maximum(old, jnp.max(score, axis=2, keepdims=True))
        terms = jnp.exp2(score - new[:, :, 0:1])
        fade = jnp.exp2(old - new)
        top[...] = new
        total[...] = total[...] * fade + jnp.sum(terms, axis=2, keepdims=True)
        more = jnp.dot(
            terms.astype(BF16).reshape(heads * tokens, 2 * tokens), vs, preferred_element_type=F32
        ).reshape(heads, tokens, HEAD)
        mixed[...] = mixed[...] * fade + more

    def attend_to(*distances):
        for d in distances:
            kv.ready(d)
            if d == 0:
                attend(x, 0)
                attend(xp, 0)
            else:
                attend(jnp.where(lax.rem(z + d + NZ, NZ) < z, x, 0), d)

    kv.tick(1)
    kv.tick(2)
    out.tick(1)
    attend_to(0)
    kv.tick(3)
    attend_to(-1, 1)
    out.tick(2)
    kv.tick(4)
    attend_to(-2, 2)
    out.tick(3)
    kv.tick(5)
    attend_to(-3, 3)
    out.tick(4)
    attend_to(-4)
    for h in range(heads):
        attended[:, h * HEAD:(h + 1) * HEAD] = (mixed[h] / total[h]).astype(BF16)
    out.tick(5)
    for d in DISTANCES:
        out.ready(d)

    per = 4 * NZ // FOLD

    def project(t):
        lhs = attended[...]
        for i in range(0, per, 2):
            rhs = pool[pl.ds(t * per + i, 2)].reshape(2 * tokens, lhs.shape[1])
            proj[t, :, i * tokens:(i + 2) * tokens] = lax.dot_general(
                lhs, rhs, NT, preferred_element_type=F32
            ).astype(BF16)

    ways = (("f+", fp, fm), ("f-", fm, fp), ("fo", fo, fo))
    project(fo)
    net.push(("p", 2), proj.at[fo], inbox.at[2], "fo")
    project(fp)
    net.push(("p", 0), proj.at[fp], inbox.at[0], "f+")
    project(fm)
    net.push(("p", 1), proj.at[fm], inbox.at[1], "f-")
    project(f)
    base = act[...].astype(F32) + proj[f].astype(F32)
    for k, way in enumerate(("f+", "f-", "fo")):
        net.await_(("p", k), inbox.at[k], way)
        base = base + inbox[k].astype(F32)
    kept = base.astype(BF16)
    resid[...] = kept
    wide = kept.astype(F32)
    stat[0] = lax.dot_general(
        jnp.ones((8, feats), F32), wide * wide, NT, preferred_element_type=F32, precision=lax.Precision.HIGHEST
    )
    for k, way in enumerate(("f+", "f-", "fo")):
        net.push(("s", k), stat.at[0], stat.at[k + 1], way)
    normed = wide * gain[...].astype(F32)
    for k, way in enumerate(("f+", "f-", "fo")):
        net.await_(("s", k), stat.at[k + 1], way)
    squares = stat[0] + stat[1] + stat[2] + stat[3]
    scale = lax.rsqrt(squares / (feats * FOLD) + EPS)
    scale = lax.dot_general(eye.astype(F32), scale, NT, preferred_element_type=F32, precision=lax.Precision.HIGHEST)
    xg[net.cp] = (normed * scale[:, 0:1]).astype(BF16)

    xs = Gather(net, "x", xg, rows1)
    xs.tick(0)
    resplit(1, wu, wuv)

    for g in range(NZ):
        for e in range(2):
            expert = (2 * net.cp + e).astype(F32)
            for k in range(4):
                meta = kvg[place(k // 2, g, k % 2), tokens:tokens + 16].astype(F32)
                chosen = meta[0:8, 0:tokens] == expert
                row = pl.ds(2 * g + e, 1)
                columns = pl.ds(k * tokens, tokens)
                hits[row, columns] = jnp.sum(jnp.where(chosen, 1.0, 0.0), axis=0, keepdims=True)
                shares = meta[8:16, 0:tokens] + meta[0:8, tokens:2 * tokens]
                share[row, columns] = jnp.sum(jnp.where(chosen, shares, 0.0), axis=0, keepdims=True)
    xs.tick(1)
    wide4 = 4 * tokens
    earlier = lax.broadcasted_iota(jnp.int32, (wide4, wide4), 0) < lax.broadcasted_iota(jnp.int32, (wide4, wide4), 1)
    hit = hits[...]
    before = jnp.dot(hit.astype(BF16), jnp.where(earlier, 1.0, 0.0).astype(BF16), preferred_element_type=F32)
    rank[...] = jnp.where(hit > 0.5, before, -1.0)

    def group(d):
        return lax.rem(z + d + NZ, NZ)

    def pick(d, e):
        row = rank[pl.ds(2 * group(d) + e, 1), :]
        want = lax.broadcasted_iota(jnp.int32, (cap, 4 * tokens), 0).astype(F32)
        return jnp.where(want == row, 1.0, 0.0)

    def select(i):
        for j, d in enumerate(STAGES[i]):
            xs.ready(d)
            g = group(d)
            low = xg[pl.ds(2 * g, 2)].reshape(2 * tokens, feats)
            high = xg[pl.ds(2 * NZ + 2 * g, 2)].reshape(2 * tokens, feats)
            choice = jnp.concatenate([pick(d, 0), pick(d, 1)], axis=0).astype(BF16)
            got = jnp.dot(choice[:, 0:2 * tokens], low, preferred_element_type=F32)
            got = (got + jnp.dot(choice[:, 2 * tokens:], high, preferred_element_type=F32)).astype(BF16)
            for e in range(2):
                slots[i, pl.ds((2 * e + j) * cap, cap), :] = got[e * cap:(e + 1) * cap]

    wide_hid = FOLD * hid

    def enter(i):
        for e in range(2):
            lhs = slots[i, pl.ds(2 * e * cap, 2 * cap), :]
            for k, w in enumerate((wgv, wuv)):
                res = lax.dot_general(lhs, w[e], NT, preferred_element_type=F32).astype(BF16)
                part[i, 2 * e, :, k * wide_hid:(k + 1) * wide_hid] = res[0:cap]
                part[i, 2 * e + 1, :, k * wide_hid:(k + 1) * wide_hid] = res[cap:]
        net.push(("a", i), part.at[i, fo, :, pl.ds(0, wide_hid)], ra.at[i], "f+")
        net.push(("b", i), part.at[i, fo, :, pl.ds(wide_hid, wide_hid)], rb.at[i], "f-")

    def relay(i):
        left, right = pl.ds(0, wide_hid), pl.ds(wide_hid, wide_hid)
        net.await_(("a", i), ra.at[i], "f+")
        part[i, fp, :, left] = (part[i, fp, :, left].astype(F32) + ra[i].astype(F32)).astype(BF16)
        net.push(("c", i), part.at[i, fp], rc.at[i], "f+")
        net.await_(("b", i), rb.at[i], "f-")
        part[i, fm, :, right] = (part[i, fm, :, right].astype(F32) + rb[i].astype(F32)).astype(BF16)
        net.push(("d", i), part.at[i, fm], rd.at[i], "f-")

    def activate(i):
        net.await_(("c", i), rc.at[i], "f+")
        net.await_(("d", i), rd.at[i], "f-")
        both = part[i, f].astype(F32) + rc[i].astype(F32) + rd[i].astype(F32)
        gate, up = both[:, 0:wide_hid], both[:, wide_hid:2 * wide_hid]
        hidden[i, f] = (gate / (1.0 + jnp.exp(-gate)) * up).astype(BF16)
        net.push(("h+", i), hidden.at[i, f], hidden.at[i, f], "f+")
        net.push(("h-", i), hidden.at[i, f], hidden.at[i, f], "f-")

    half_hid = wide_hid // 2

    def spread(i):
        net.await_(("h+", i), hidden.at[i, fm], "f+")
        lower = hidden.at[i, fm, :, pl.ds(0, half_hid)]
        net.push(("i+", i), lower, lower, "f+")
        net.await_(("h-", i), hidden.at[i, fp], "f-")
        upper = hidden.at[i, fp, :, pl.ds(half_hid, half_hid)]
        net.push(("i-", i), upper, upper, "f-")

    def leave(i):
        net.await_(("i+", i), hidden.at[i, fo, :, pl.ds(0, half_hid)], "f+")
        net.await_(("i-", i), hidden.at[i, fo, :, pl.ds(half_hid, half_hid)], "f-")
        for e in range(2):
            lhs = hidden[i, 2 * e:2 * e + 2].reshape(2 * cap, wide_hid)
            res = jnp.dot(lhs, wdv[e], preferred_element_type=F32)
            for j, d in enumerate(STAGES[i]):
                row = share[pl.ds(2 * group(d) + e, 1), :]
                scaled = jnp.sum(pick(d, e) * row, axis=1, keepdims=True)
                result[2 * j + e] = (res[j * cap:(j + 1) * cap] * scaled).astype(BF16)
        for j, d in enumerate(STAGES[i]):
            g = group(d)
            choice = jnp.concatenate([pick(d, 0), pick(d, 1)], axis=0).astype(BF16)
            res = result[2 * j:2 * j + 2].reshape(2 * cap, feats)
            summed = lax.dot_general(choice, res, (((0,), (0,)), ((), ())), preferred_element_type=F32).astype(BF16)
            for k in range(4):
                pool[place(k // 2, g, k % 2)] = summed[k * tokens:(k + 1) * tokens]
            for xx in range(2):
                net.push(("rc", d, xx), pool.at[place(xx, g, cpeer)], cin.at[g, xx], "c")

    def accumulate(at, rows, inc):
        pool[at, rows] = (pool[at, rows].astype(F32) + inc.astype(F32)).astype(BF16)

    full, ahead, rest = pl.ds(0, tokens), pl.ds(0, rows1), pl.ds(rows1, rows2)

    def merge(i):
        for d in STAGES[i]:
            g = group(d)
            for xx in range(2):
                net.await_(("rc", d, xx), cin.at[g, xx], "c")
                accumulate(place(xx, g, c), full, cin[g, xx])
            net.push(("rx", d), pool.at[place(xp, g, c), ahead], xin.at[g], "x")

    def cross(d):
        g = group(d)
        net.await_(("rx", d), xin.at[g], "x")
        accumulate(place(x, g, c), ahead, xin[g])

    lines = (
        ("z-", -1, 4, x, zin, 0, full),
        ("z+", 1, 3, x, zin, 4, full),
        ("z-", -1, 3, xp, yin, 0, rest),
        ("z+", 1, 4, xp, yin, 3, rest),
    )

    def hop(k, d):
        way, sign, hops, line, inbox, first, rows = lines[k]
        s = hops - abs(d)
        at = place(line, z + d, c)
        if s > 0:
            net.await_(("rz", k, s - 1), inbox.at[first + s - 1], way)
            accumulate(at, rows, inbox[first + s - 1])
        if s < hops:
            net.push(("rz", k, s), pool.at[at, rows], inbox.at[first + s], way)

    xs.tick(2)
    xs.tick(3)
    select(3)
    xs.tick(4)
    select(2)
    xs.tick(5)
    select(1)
    select(0)
    net.drain("wo")
    for k, dst in enumerate((wgv, wuv)):
        for way, t in (("f+", fm), ("f-", fp), ("fo", fo)):
            net.await_(("w", k, way), dst.at[:, pl.ds(t * hid, hid), :], way)
    for copy in loads:
        copy.wait()

    enter(0)
    enter(1)
    relay(0)
    relay(1)
    activate(0)
    enter(2)
    activate(1)
    spread(0)
    relay(2)
    leave(0)
    spread(1)
    enter(3)
    activate(2)
    merge(0)
    leave(1)
    relay(3)
    spread(2)
    cross(-4)
    hop(0, -4)
    hop(3, 4)
    cross(3)
    hop(1, 3)
    merge(1)
    activate(3)
    leave(2)
    cross(-3)
    hop(0, -3)
    hop(2, -3)
    hop(3, 3)
    cross(2)
    spread(3)
    hop(1, 2)
    merge(2)
    hop(3, 2)
    leave(3)
    cross(1)
    hop(1, 1)
    hop(3, 1)
    cross(-2)
    hop(0, -2)
    hop(2, -2)
    merge(3)
    cross(-1)
    hop(0, -1)
    hop(2, -1)
    cross(0)
    hop(3, 0)
    hop(1, 0)
    hop(2, 0)
    net.push(("rt",), pool.at[place(xp, z, c), rest], tin, "x")
    hop(0, 0)
    own = resid[...].astype(F32) + pool[net.cp].astype(F32)
    done[ahead] = own[0:rows1].astype(BF16)
    net.push(("out", 0), done.at[ahead], passed.at[ahead], "sec")
    net.await_(("rt",), tin, "x")
    done[rest] = (own[rows1:] + tin[...].astype(F32)).astype(BF16)
    net.push(("out", 1), done.at[rest], passed.at[rest], "sec")
    net.await_(("seg",), passed_segments, "sec")
    net.await_(("out", 0), passed.at[ahead], "sec")
    net.await_(("out", 1), passed.at[rest], "sec")
    net.drain()


def run_layer(q, keys, values, segments, routes, weights, act, gain, wo, wg, wu, wd):
    tokens, feats = act.shape
    blocks = 4 * NZ
    experts, quarter, wide = wg.shape
    hid = quarter * FOLD
    cap = 4 * CAP
    heads = q.shape[1] // HEAD
    rows1 = tokens * 5 // 8
    dma = pltpu.SemaphoreType.DMA

    def scratch(*shape, dtype=BF16):
        return pltpu.VMEM(shape, dtype)

    vmem, hbm = pl.BlockSpec(memory_space=pltpu.VMEM), pl.BlockSpec(memory_space=pl.ANY)
    return pl.pallas_call(
        layer,
        out_shape=(jax.ShapeDtypeStruct((tokens, feats), BF16), jax.ShapeDtypeStruct(segments.shape, segments.dtype)),
        in_specs=[vmem] * 9 + [hbm] * 3,
        out_specs=(vmem, vmem),
        scratch_shapes=[
            scratch(blocks, tokens + 16, 2 * HEAD),
            scratch(blocks, tokens, feats),
            scratch(blocks, tokens, feats),
            scratch(experts, hid, feats),
            scratch(experts, hid, feats),
            scratch(experts, hid, feats),
            scratch(heads, tokens, HEAD),
            scratch(heads, tokens, HEAD, dtype=F32),
            scratch(heads, tokens, HEAD, dtype=F32),
            scratch(heads, tokens, HEAD, dtype=F32),
            scratch(*q.shape),
            scratch(2 * NZ, 4 * tokens, dtype=F32),
            scratch(2 * NZ, 4 * tokens, dtype=F32),
            scratch(2 * NZ, 4 * tokens, dtype=F32),
            scratch(FOLD, tokens, feats),
            scratch(3, tokens, feats),
            scratch(4, 8, tokens, dtype=F32),
            scratch(4, 4 * cap, feats),
            scratch(4, FOLD, cap, 2 * hid),
            scratch(4, cap, hid),
            scratch(4, cap, hid),
            scratch(4, cap, 2 * hid),
            scratch(4, cap, 2 * hid),
            scratch(4, FOLD, cap, hid),
            scratch(4, cap, feats),
            scratch(NZ, 2, tokens, feats),
            scratch(NZ, rows1, feats),
            scratch(7, tokens, feats),
            scratch(7, tokens - rows1, feats),
            scratch(tokens - rows1, feats),
            scratch(tokens, feats),
            scratch(tokens, feats),
            dma((224,)),
            dma((224,)),
            dma((3,)),
        ],
        compiler_params=pltpu.CompilerParams(collective_id=0, has_side_effects=True, vmem_limit_bytes=62 * 2**20),
        name="layer",
    )(q, keys, values, segments, routes, weights, act, gain, wo, wg, wu, wd)


def body(
    activations, queries, keys, values, segments, routes, route_weight, norm_gain, w_out, w_gate, w_up, w_down,
):
    passed, moved = run_layer(
        queries[0], keys[0], values[0], segments, routes[0].T, route_weight[0].T, activations[0], norm_gain,
        w_out[0], w_gate[0], w_up[0], w_down[0],
    )
    return passed[None], moved


def solution(mesh):
    return jax.shard_map(
        body,
        mesh=mesh,
        in_specs=(
            P("section", "cp", "fold"),
            P("section", "cp", "fold"),
            P("section", "cp", "fold"),
            P("section", "cp", "fold"),
            P("section", "cp"),
            P("section", "cp", None),
            P("section", "cp", None),
            P("section", "fold"),
            P("section", "fold", "cp"),
            P("section", "cp", "fold", None),
            P("section", "cp", "fold", None),
            P("section", "cp", None, "fold"),
        ),
        out_specs=(P("section", "cp", "fold"), P("section", "cp")),
        check_vma=False,
    )
```

```python
import math

import jax
import jax.numpy as jnp
from jax import lax
from jax.experimental import pallas as pl
from jax.experimental.pallas import tpu as pltpu
from jax.sharding import PartitionSpec as P

MESH = pl.DeviceIdType.MESH
HEAD = 128
NZ = 8
FOLD = 4
NEG = -1e30
EPS = 1e-06
CAP = 20
F32 = jnp.float32
BF16 = jnp.bfloat16


def place(x, z, c):
    return x * (2 * NZ) + lax.rem(z + 2 * NZ, NZ) * 2 + c


class Net:
    def __init__(self, send, recv):
        self.send_sems, self.recv_sems = send, recv
        cp = lax.axis_index("cp")
        self.cp = cp
        self.x = cp // (2 * NZ)
        self.z = (cp // 2) % NZ
        self.c = cp % 2
        self.f = lax.axis_index("fold")
        self.xp = 1 - self.x
        self.fp, self.fo, self.fm = [lax.rem(self.f + k, FOLD) for k in (1, 2, 3)]
        self.ids = {}
        self.sent = []

    def to(self, way):
        x, z, c = self.x, self.z, self.c
        if way == "z+":
            return {"cp": place(x, z + 1, c)}
        if way == "z-":
            return {"cp": place(x, z - 1, c)}
        if way == "x":
            return {"cp": place(1 - x, z, c)}
        if way == "c":
            return {"cp": place(x, z, 1 - c)}
        if way == "f+":
            return {"fold": self.fp}
        if way == "f-":
            return {"fold": self.fm}
        if way == "fo":
            return {"fold": self.fo}
        return {"section": 1 - lax.axis_index("section")}

    def greet(self, ways):
        for way in ways:
            pl.semaphore_signal(
                pltpu.get_barrier_semaphore(), inc=1, device_id=self.to(way), device_id_type=MESH
            )

    def meet(self, ways):
        pl.semaphore_wait(pltpu.get_barrier_semaphore(), len(ways))

    def slot(self, name):
        return self.ids.setdefault(name, len(self.ids))

    def copy(self, name, src, dst, way):
        i = self.slot(name)
        return pltpu.make_async_remote_copy(
            src_ref=src,
            dst_ref=dst,
            send_sem=self.send_sems.at[i],
            recv_sem=self.recv_sems.at[i],
            device_id=self.to(way),
            device_id_type=MESH,
        )

    def push(self, name, src, dst, way):
        copy = self.copy(name, src, dst, way)
        copy.start()
        self.sent.append((name[0], copy))

    def await_(self, name, dst, way):
        self.copy(name, dst, dst, way).wait_recv()

    def drain(self, *kinds):
        for kind, copy in self.sent:
            if not kinds or kind in kinds:
                copy.wait_send()
        self.sent = [entry for entry in self.sent if kinds and entry[0] not in kinds]


class Gather:
    def __init__(self, net, name, buf, rows1):
        self.net, self.name, self.buf = net, name, buf
        self.rows = buf.shape[1]
        self.rows1 = rows1

    def block(self, x, z, c, part="full"):
        ref = self.buf.at[place(x, z, c)]
        if part == "full":
            return ref
        if part == "r1":
            return ref.at[pl.ds(0, self.rows1)]
        return ref.at[pl.ds(self.rows1, self.rows - self.rows1)]

    def push(self, tag, key, way, part="full"):
        ref = self.block(*key, part)
        self.net.push((self.name, tag), ref, ref, way)

    def wait(self, tag, key, way, part="full"):
        self.net.await_((self.name, tag), self.block(*key, part), way)

    def tick(self, s):
        n = self.net
        x, z, c, xp, cp = n.x, n.z, n.c, n.xp, 1 - n.c
        if s == 0:
            for tag, way in (("zp0", "z+"), ("zm0", "z-"), ("x0", "x"), ("c0", "c")):
                self.push(tag, (x, z, c), way)
            return
        if s == 1:
            self.wait("x0", (xp, z, c), "x")
            self.push("yp0", (xp, z, c), "z+", "r2")
            self.push("ym0", (xp, z, c), "z-", "r2")
            self.push("cx0", (xp, z, c), "c")
        if s <= 4:
            near = "full" if s <= 3 else "r1"
            self.wait(f"zp{s - 1}", (x, z - s, c), "z+", near)
            if s <= 3:
                self.push(f"zp{s}", (x, z - s, c), "z+", "full" if s <= 2 else "r1")
                self.wait(f"zm{s - 1}", (x, z + s, c), "z-")
                self.push(f"zm{s}", (x, z + s, c), "z-", "full" if s <= 2 else "r2")
            self.push(f"xm{s}", (x, z - s, c), "x", "r1")
            if s <= 3:
                self.push(f"xp{s}", (x, z + s, c), "x", "r1")
            self.push(f"cm{s}", (x, z - s, c), "c", near)
            if s <= 3:
                self.push(f"cp{s}", (x, z + s, c), "c")
            else:
                self.wait("zm3", (x, z + 4, c), "z-", "r2")
                self.push("cn4", (x, z + 4, c), "c", "r2")
        if s >= 2 and s <= 5:
            d = s - 1
            self.wait(f"ym{d - 1}", (xp, z + d, c), "z-", "r2")
            if d <= 3:
                self.push(f"ym{d}", (xp, z + d, c), "z-", "r2")
                self.wait(f"yp{d - 1}", (xp, z - d, c), "z+", "r2")
                if d <= 2:
                    self.push(f"yp{d}", (xp, z - d, c), "z+", "r2")
            self.push(f"dp{d}", (xp, z + d, c), "c", "r2")
            if d <= 3:
                self.push(f"dm{d}", (xp, z - d, c), "c", "r2")
            self.wait(f"xm{d}", (xp, z - d, c), "x", "r1")
            self.push(f"em{d}", (xp, z - d, c), "c", "r1")
            if d <= 3:
                self.wait(f"xp{d}", (xp, z + d, c), "x", "r1")
                self.push(f"ep{d}", (xp, z + d, c), "c", "r1")

    def ready(self, d):
        n = self.net
        x, z, xp, cp = n.x, n.z, n.xp, 1 - n.c
        if d == 0:
            self.wait("c0", (x, z, cp), "c")
            self.wait("cx0", (xp, z, cp), "c")
            return
        side, s = ("p", d) if d > 0 else ("m", -d)
        self.wait(f"c{side}{s}", (x, z + d, cp), "c", "full" if s <= 3 else "r1")
        if s == 4:
            self.wait("cn4", (x, z + d, cp), "c", "r2")
        self.wait(f"d{'p' if s == 4 else side}{s}", (xp, z + d, cp), "c", "r2")
        self.wait(f"e{side}{s}", (xp, z + d, cp), "c", "r1")


DISTANCES = (0, -1, 1, -2, 2, -3, 3, -4)
STAGES = ((3, -4), (2, -3), (1, -2), (-1, 0))
WAYS = ("z+", "z-", "x", "c", "f+", "f-", "fo", "sec")
NT = (((1,), (1,)), ((), ()))


def layer(
    q, keys, values, segments, routes, weights, act, gain, wo, wg, wu, wd,
    passed, passed_segments,
    kvg, pool, xg, wgv, wuv, wdv, qs, top, total, mixed, attended, hits, rank, share, proj, mine, inbox, stat,
    slots, part, ra, rb, rc, rd, hidden, result, cin, xin, zin, yin, tin, resid, done,
    send, recv, pair_send, pair_recv, local,
):
    net = Net(send, recv)
    x, z, c, xp, cpeer = net.x, net.z, net.c, net.xp, 1 - net.c
    f, fp, fo, fm = net.f, net.fp, net.fo, net.fm
    tokens, feats = act.shape
    cap = 4 * CAP
    rows1 = tokens * 5 // 8
    rows2 = tokens - rows1
    net.greet(WAYS)

    kvg[net.cp, 0:tokens, 0:HEAD] = keys[...]
    kvg[net.cp, 0:tokens, HEAD:2 * HEAD] = values[...]
    weight = weights[...]
    coarse = weight.astype(BF16).astype(F32)
    side = jnp.broadcast_to(segments[...].astype(F32), (8, tokens))
    meta = jnp.concatenate([routes[...].astype(F32), coarse], axis=0)
    kvg[net.cp, tokens:tokens + 16, 0:HEAD] = meta.astype(BF16)
    meta = jnp.concatenate([weight - coarse, side], axis=0)
    kvg[net.cp, tokens:tokens + 16, HEAD:2 * HEAD] = meta.astype(BF16)
    eye = (
        lax.broadcasted_iota(jnp.int32, (tokens, tokens), 0) == lax.broadcasted_iota(jnp.int32, (tokens, tokens), 1)
    ).astype(F32).astype(BF16)
    seg_q = lax.dot_general(eye, jnp.concatenate([side, side], axis=0).astype(BF16), NT, preferred_element_type=F32)[:, 0:1]
    pool[net.cp] = lax.dot_general(eye, wo[...], NT, preferred_element_type=F32).astype(BF16)

    net.meet(WAYS)
    kv = Gather(net, "kv", kvg, rows1)
    out = Gather(net, "wo", pool, rows1)
    kv.tick(0)
    out.tick(0)
    hid = wg.shape[1]
    loads = [pltpu.make_async_copy(wd, wdv, local.at[2])]
    for k, (src, dst) in enumerate(((wg, wgv), (wu, wuv))):
        rows = pl.ds(f * hid, hid)
        loads.append(
            pltpu.make_async_copy(src.at[:, :, pl.ds(f * feats, feats)], dst.at[:, rows, :], local.at[k])
        )
    for copy in loads:
        copy.start()

    def resplit(k, src, dst):
        for way, t in (("f+", fp), ("f-", fm), ("fo", fo)):
            net.push(("w", k, way), src.at[:, :, pl.ds(t * feats, feats)], dst.at[:, pl.ds(f * hid, hid), :], way)

    resplit(0, wg, wgv)
    net.push(("seg",), segments, passed_segments, "sec")

    heads = q.shape[1] // HEAD
    for h in range(heads):
        qs[h] = q[:, h * HEAD:(h + 1) * HEAD]
    top[...] = jnp.full(top.shape, NEG, F32)
    total[...] = jnp.zeros(total.shape, F32)
    mixed[...] = jnp.zeros(mixed.shape, F32)
    factor = math.log2(math.e) / math.sqrt(HEAD)
    q_place = net.cp * tokens + lax.broadcasted_iota(jnp.int32, (tokens, 2 * tokens), 0)

    def attend(line, d):
        base = place(line, z + d, 0)
        ks = kvg[pl.ds(base, 2), 0:tokens, 0:HEAD].reshape(2 * tokens, HEAD)
        vs = kvg[pl.ds(base, 2), 0:tokens, HEAD:2 * HEAD].reshape(2 * tokens, HEAD)
        seg_k = jnp.concatenate(
            [kvg[base + i, tokens:tokens + 16, HEAD:2 * HEAD].astype(F32)[8:9] for i in range(2)], axis=1
        )
        k_place = base * tokens + lax.broadcasted_iota(jnp.int32, (tokens, 2 * tokens), 1)
        bias = jnp.where((k_place <= q_place) & (seg_k == seg_q), 0.0, NEG)
        score = lax.dot_general(qs[...].reshape(heads * tokens, HEAD), ks, NT, preferred_element_type=F32)
        score = score.reshape(heads, tokens, 2 * tokens) * factor + bias[None]
        old = top[...]
        new = jnp.maximum(old, jnp.max(score, axis=2, keepdims=True))
        terms = jnp.exp2(score - new[:, :, 0:1])
        fade = jnp.exp2(old - new)
        top[...] = new
        total[...] = total[...] * fade + jnp.sum(terms, axis=2, keepdims=True)
        more = jnp.dot(
            terms.astype(BF16).reshape(heads * tokens, 2 * tokens), vs, preferred_element_type=F32
        ).reshape(heads, tokens, HEAD)
        mixed[...] = mixed[...] * fade + more

    def attend_to(*distances):
        for d in distances:
            kv.ready(d)
            if d == 0:
                attend(x, 0)
                attend(xp, 0)
            else:
                attend(jnp.where(lax.rem(z + d + NZ, NZ) < z, x, 0), d)

    kv.tick(1)
    kv.tick(2)
    attend_to(0)
    kv.tick(3)
    out.tick(1)
    attend_to(-1, 1)
    kv.tick(4)
    out.tick(2)
    attend_to(-2, 2)
    kv.tick(5)
    attend_to(-3, 3)
    out.tick(3)
    attend_to(-4)
    for h in range(heads):
        attended[:, h * HEAD:(h + 1) * HEAD] = (mixed[h] / total[h]).astype(BF16)

    pairs = [(line, d) for d in DISTANCES for line in range(2)]
    per = 4 * NZ // FOLD
    two = 2 * tokens

    def owner(line, d):
        base = place(line, z + d, 0)
        t = base // per
        return base, lax.rem(t - f + FOLD, FOLD), base % per

    def shipment(n, line, d):
        base, k, column = owner(line, d)
        return pltpu.make_async_remote_copy(
            src_ref=proj.at[n],
            dst_ref=inbox.at[k - 1, :, pl.ds(pl.multiple_of(column * tokens, two), two)],
            send_sem=pair_send.at[n],
            recv_sem=pair_recv.at[(k - 1) * 4 + column // 2],
            device_id={"fold": base // per},
            device_id_type=MESH,
        )

    def project_to(*distances):
        for d in distances:
            out.ready(d)
            for line in range(2):
                n = pairs.index((line, d))
                base, k, column = owner(line, d)
                rhs = pool[pl.ds(base, 2)].reshape(two, attended.shape[1])
                res = lax.dot_general(attended[...], rhs, NT, preferred_element_type=F32).astype(BF16)
                proj[n] = res

                @pl.when(k == 0)
                def _():
                    mine[:, pl.ds(pl.multiple_of(column * tokens, two), two)] = res

                @pl.when(k != 0)
                def _():
                    shipment(n, line, d).start()

    project_to(0, -1, 1)
    out.tick(4)
    project_to(-2, 2)
    out.tick(5)
    project_to(-3, 3, -4)
    base = act[...].astype(F32) + mine[...].astype(F32)
    for k in range(3):
        for j in range(4):
            block = inbox.at[k, :, pl.ds(j * two, two)]
            pltpu.make_async_remote_copy(
                src_ref=block,
                dst_ref=block,
                send_sem=pair_send.at[0],
                recv_sem=pair_recv.at[k * 4 + j],
                device_id={"fold": fp},
                device_id_type=MESH,
            ).wait_recv()
        base = base + inbox[k].astype(F32)
    kept = base.astype(BF16)
    resid[...] = kept
    wide = kept.astype(F32)
    stat[0] = lax.dot_general(
        jnp.ones((8, feats), F32), wide * wide, NT, preferred_element_type=F32, precision=lax.Precision.HIGHEST
    )
    for k, way in enumerate(("f+", "f-", "fo")):
        net.push(("s", k), stat.at[0], stat.at[k + 1], way)
    normed = wide * gain[...].astype(F32)
    for k, way in enumerate(("f+", "f-", "fo")):
        net.await_(("s", k), stat.at[k + 1], way)
    squares = stat[0] + stat[1] + stat[2] + stat[3]
    scale = lax.rsqrt(squares / (feats * FOLD) + EPS)
    scale = lax.dot_general(eye.astype(F32), scale, NT, preferred_element_type=F32, precision=lax.Precision.HIGHEST)
    xg[net.cp] = (normed * scale[:, 0:1]).astype(BF16)

    xs = Gather(net, "x", xg, rows1)
    xs.tick(0)
    resplit(1, wu, wuv)

    for g in range(NZ):
        for e in range(2):
            expert = (2 * net.cp + e).astype(F32)
            for k in range(4):
                meta = kvg[place(k // 2, g, k % 2), tokens:tokens + 16].astype(F32)
                chosen = meta[0:8, 0:tokens] == expert
                row = pl.ds(2 * g + e, 1)
                columns = pl.ds(k * tokens, tokens)
                hits[row, columns] = jnp.sum(jnp.where(chosen, 1.0, 0.0), axis=0, keepdims=True)
                shares = meta[8:16, 0:tokens] + meta[0:8, tokens:2 * tokens]
                share[row, columns] = jnp.sum(jnp.where(chosen, shares, 0.0), axis=0, keepdims=True)
    xs.tick(1)
    wide4 = 4 * tokens
    earlier = lax.broadcasted_iota(jnp.int32, (wide4, wide4), 0) < lax.broadcasted_iota(jnp.int32, (wide4, wide4), 1)
    hit = hits[...]
    before = jnp.dot(hit.astype(BF16), jnp.where(earlier, 1.0, 0.0).astype(BF16), preferred_element_type=F32)
    rank[...] = jnp.where(hit > 0.5, before, -1.0)

    def group(d):
        return lax.rem(z + d + NZ, NZ)

    def pick(d, e):
        row = rank[pl.ds(2 * group(d) + e, 1), :]
        want = lax.broadcasted_iota(jnp.int32, (cap, 4 * tokens), 0).astype(F32)
        return jnp.where(want == row, 1.0, 0.0)

    def select(i):
        for j, d in enumerate(STAGES[i]):
            xs.ready(d)
            g = group(d)
            low = xg[pl.ds(2 * g, 2)].reshape(2 * tokens, feats)
            high = xg[pl.ds(2 * NZ + 2 * g, 2)].reshape(2 * tokens, feats)
            choice = jnp.concatenate([pick(d, 0), pick(d, 1)], axis=0).astype(BF16)
            got = jnp.dot(choice[:, 0:2 * tokens], low, preferred_element_type=F32)
            got = (got + jnp.dot(choice[:, 2 * tokens:], high, preferred_element_type=F32)).astype(BF16)
            for e in range(2):
                slots[i, pl.ds((2 * e + j) * cap, cap), :] = got[e * cap:(e + 1) * cap]

    wide_hid = FOLD * hid

    def enter(i, k):
        w = (wgv, wuv)[k]
        columns = pl.ds(k * wide_hid, wide_hid)
        for e in range(2):
            lhs = slots[i, pl.ds(2 * e * cap, 2 * cap), :]
            res = lax.dot_general(lhs, w[e], NT, preferred_element_type=F32).astype(BF16)
            part[i, 2 * e, :, columns] = res[0:cap]
            part[i, 2 * e + 1, :, columns] = res[cap:]
        if k == 0:
            net.push(("a", i), part.at[i, fo, :, columns], ra.at[i], "f+")
        else:
            net.push(("b", i), part.at[i, fo, :, columns], rb.at[i], "f-")

    def have(k):
        dst = (wgv, wuv)[k]
        for way, t in (("f+", fm), ("f-", fp), ("fo", fo)):
            net.await_(("w", k, way), dst.at[:, pl.ds(t * hid, hid), :], way)
        loads[k + 1].wait()

    def relay(i):
        left, right = pl.ds(0, wide_hid), pl.ds(wide_hid, wide_hid)
        net.await_(("a", i), ra.at[i], "f+")
        part[i, fp, :, left] = (part[i, fp, :, left].astype(F32) + ra[i].astype(F32)).astype(BF16)
        net.push(("c", i), part.at[i, fp], rc.at[i], "f+")
        net.await_(("b", i), rb.at[i], "f-")
        part[i, fm, :, right] = (part[i, fm, :, right].astype(F32) + rb[i].astype(F32)).astype(BF16)
        net.push(("d", i), part.at[i, fm], rd.at[i], "f-")

    def activate(i):
        net.await_(("c", i), rc.at[i], "f+")
        net.await_(("d", i), rd.at[i], "f-")
        both = part[i, f].astype(F32) + rc[i].astype(F32) + rd[i].astype(F32)
        gate, up = both[:, 0:wide_hid], both[:, wide_hid:2 * wide_hid]
        hidden[i, f] = (gate / (1.0 + jnp.exp(-gate)) * up).astype(BF16)
        net.push(("h+", i), hidden.at[i, f], hidden.at[i, f], "f+")
        net.push(("h-", i), hidden.at[i, f], hidden.at[i, f], "f-")

    half_hid = wide_hid // 2

    def spread(i):
        net.await_(("h+", i), hidden.at[i, fm], "f+")
        lower = hidden.at[i, fm, :, pl.ds(0, half_hid)]
        net.push(("i+", i), lower, lower, "f+")
        net.await_(("h-", i), hidden.at[i, fp], "f-")
        upper = hidden.at[i, fp, :, pl.ds(half_hid, half_hid)]
        net.push(("i-", i), upper, upper, "f-")

    def leave(i):
        net.await_(("i+", i), hidden.at[i, fo, :, pl.ds(0, half_hid)], "f+")
        net.await_(("i-", i), hidden.at[i, fo, :, pl.ds(half_hid, half_hid)], "f-")
        for group_ids in ((0, 1),) if i < 3 else ((0,), (1,)):
            for e in range(2):
                lhs = hidden[i, pl.ds(2 * e + group_ids[0], len(group_ids))].reshape(len(group_ids) * cap, wide_hid)
                res = jnp.dot(lhs, wdv[e], preferred_element_type=F32)
                for n, j in enumerate(group_ids):
                    d = STAGES[i][j]
                    row = share[pl.ds(2 * group(d) + e, 1), :]
                    scaled = jnp.sum(pick(d, e) * row, axis=1, keepdims=True)
                    result[2 * j + e] = (res[n * cap:(n + 1) * cap] * scaled).astype(BF16)
            for j in group_ids:
                d = STAGES[i][j]
                g = group(d)
                choice = jnp.concatenate([pick(d, 0), pick(d, 1)], axis=0).astype(BF16)
                res = result[2 * j:2 * j + 2].reshape(2 * cap, feats)
                summed = lax.dot_general(
                    choice, res, (((0,), (0,)), ((), ())), preferred_element_type=F32
                ).astype(BF16)
                for k in range(4):
                    pool[place(k // 2, g, k % 2)] = summed[k * tokens:(k + 1) * tokens]
                for xx in range(2):
                    net.push(("rc", d, xx), pool.at[place(xx, g, cpeer)], cin.at[g, xx], "c")

    def accumulate(at, rows, inc):
        pool[at, rows] = (pool[at, rows].astype(F32) + inc.astype(F32)).astype(BF16)

    full, ahead, rest = pl.ds(0, tokens), pl.ds(0, rows1), pl.ds(rows1, rows2)

    def merge(*distances):
        for d in distances:
            g = group(d)
            for xx in range(2):
                net.await_(("rc", d, xx), cin.at[g, xx], "c")
                accumulate(place(xx, g, c), full, cin[g, xx])
            net.push(("rx", d), pool.at[place(xp, g, c), ahead], xin.at[g], "x")

    def cross(d):
        g = group(d)
        net.await_(("rx", d), xin.at[g], "x")
        accumulate(place(x, g, c), ahead, xin[g])

    lines = (
        ("z-", -1, 4, x, zin, 0, ahead),
        ("z+", 1, 3, x, zin, 4, ahead),
        ("z-", -1, 3, x, yin, 0, rest),
        ("z+", 1, 4, x, yin, 3, rest),
        ("z-", -1, 3, xp, yin, 7, rest),
        ("z+", 1, 4, xp, yin, 10, rest),
    )

    def hop(k, d):
        way, sign, hops, line, inbox, first, rows = lines[k]
        s = hops - abs(d)
        at = place(line, z + d, c)
        if s > 0:
            net.await_(("rz", k, s - 1), inbox.at[first + s - 1], way)
            accumulate(at, rows, inbox[first + s - 1])
        if s < hops:
            net.push(("rz", k, s), pool.at[at, rows], inbox.at[first + s], way)

    xs.tick(2)
    xs.tick(3)
    select(3)
    xs.tick(4)
    select(2)
    have(0)
    xs.tick(5)
    select(1)
    select(0)
    net.drain("wo")
    enter(0, 0)
    enter(1, 0)
    have(1)
    loads[0].wait()
    enter(0, 1)
    enter(1, 1)
    relay(0)
    relay(1)
    activate(0)
    enter(2, 0)
    enter(2, 1)
    activate(1)
    spread(0)
    relay(2)
    leave(0)
    spread(1)
    enter(3, 0)
    enter(3, 1)
    activate(2)
    merge(-4, 3)
    hop(3, 4)
    hop(5, 4)
    leave(1)
    relay(3)
    spread(2)
    cross(-4)
    hop(0, -4)
    cross(3)
    hop(1, 3)
    merge(-3, 2)
    hop(2, -3)
    hop(4, -3)
    activate(3)
    leave(2)
    hop(3, 3)
    hop(5, 3)
    cross(-3)
    hop(0, -3)
    cross(2)
    spread(3)
    hop(1, 2)
    merge(-2, 1)
    hop(2, -2)
    hop(4, -2)
    hop(3, 2)
    hop(5, 2)
    leave(3)
    cross(1)
    cross(-2)
    hop(0, -2)
    hop(1, 1)
    hop(3, 1)
    hop(5, 1)
    merge(-1)
    hop(2, -1)
    hop(4, -1)
    cross(-1)
    hop(0, -1)
    merge(0)
    hop(5, 0)
    hop(4, 0)
    net.push(("rt",), pool.at[place(xp, z, c), rest], tin, "x")
    hop(3, 0)
    hop(2, 0)
    cross(0)
    hop(1, 0)
    hop(0, 0)
    own = resid[...].astype(F32) + pool[net.cp].astype(F32)
    done[ahead] = own[0:rows1].astype(BF16)
    net.push(("out", 0), done.at[ahead], passed.at[ahead], "sec")
    net.await_(("rt",), tin, "x")
    done[rest] = (own[rows1:] + tin[...].astype(F32)).astype(BF16)
    net.push(("out", 1), done.at[rest], passed.at[rest], "sec")
    net.await_(("seg",), passed_segments, "sec")
    net.await_(("out", 0), passed.at[ahead], "sec")
    net.await_(("out", 1), passed.at[rest], "sec")
    net.drain()
    for n, (line, d) in enumerate(pairs):
        @pl.when(owner(line, d)[1] != 0)
        def _():
            shipment(n, line, d).wait_send()


def run_layer(q, keys, values, segments, routes, weights, act, gain, wo, wg, wu, wd):
    tokens, feats = act.shape
    blocks = 4 * NZ
    experts, quarter, wide = wg.shape
    hid = quarter * FOLD
    cap = 4 * CAP
    heads = q.shape[1] // HEAD
    rows1 = tokens * 5 // 8
    dma = pltpu.SemaphoreType.DMA

    def scratch(*shape, dtype=BF16):
        return pltpu.VMEM(shape, dtype)

    vmem, hbm = pl.BlockSpec(memory_space=pltpu.VMEM), pl.BlockSpec(memory_space=pl.ANY)
    return pl.pallas_call(
        layer,
        out_shape=(jax.ShapeDtypeStruct((tokens, feats), BF16), jax.ShapeDtypeStruct(segments.shape, segments.dtype)),
        in_specs=[vmem] * 9 + [hbm] * 3,
        out_specs=(vmem, vmem),
        scratch_shapes=[
            scratch(blocks, tokens + 16, 2 * HEAD),
            scratch(blocks, tokens, feats),
            scratch(blocks, tokens, feats),
            scratch(experts, hid, feats),
            scratch(experts, hid, feats),
            scratch(experts, hid, feats),
            scratch(heads, tokens, HEAD),
            scratch(heads, tokens, HEAD, dtype=F32),
            scratch(heads, tokens, HEAD, dtype=F32),
            scratch(heads, tokens, HEAD, dtype=F32),
            scratch(*q.shape),
            scratch(2 * NZ, 4 * tokens, dtype=F32),
            scratch(2 * NZ, 4 * tokens, dtype=F32),
            scratch(2 * NZ, 4 * tokens, dtype=F32),
            scratch(2 * NZ, tokens, 2 * tokens),
            scratch(tokens, feats),
            scratch(3, tokens, feats),
            scratch(4, 8, tokens, dtype=F32),
            scratch(4, 4 * cap, feats),
            scratch(4, FOLD, cap, 2 * hid),
            scratch(4, cap, hid),
            scratch(4, cap, hid),
            scratch(4, cap, 2 * hid),
            scratch(4, cap, 2 * hid),
            scratch(4, FOLD, cap, hid),
            scratch(4, cap, feats),
            scratch(NZ, 2, tokens, feats),
            scratch(NZ, rows1, feats),
            scratch(7, rows1, feats),
            scratch(14, tokens - rows1, feats),
            scratch(tokens - rows1, feats),
            scratch(tokens, feats),
            scratch(tokens, feats),
            dma((240,)),
            dma((240,)),
            dma((2 * NZ,)),
            dma((12,)),
            dma((3,)),
        ],
        compiler_params=pltpu.CompilerParams(collective_id=0, has_side_effects=True, vmem_limit_bytes=62 * 2**20),
        name="layer",
    )(q, keys, values, segments, routes, weights, act, gain, wo, wg, wu, wd)


def body(
    activations, queries, keys, values, segments, routes, route_weight, norm_gain, w_out, w_gate, w_up, w_down,
):
    passed, moved = run_layer(
        queries[0], keys[0], values[0], segments, routes[0].T, route_weight[0].T, activations[0], norm_gain,
        w_out[0], w_gate[0], w_up[0], w_down[0],
    )
    return passed[None], moved


def solution(mesh):
    return jax.shard_map(
        body,
        mesh=mesh,
        in_specs=(
            P("section", "cp", "fold"),
            P("section", "cp", "fold"),
            P("section", "cp", "fold"),
            P("section", "cp", "fold"),
            P("section", "cp"),
            P("section", "cp", None),
            P("section", "cp", None),
            P("section", "fold"),
            P("section", "fold", "cp"),
            P("section", "cp", "fold", None),
            P("section", "cp", "fold", None),
            P("section", "cp", None, "fold"),
        ),
        out_specs=(P("section", "cp", "fold"), P("section", "cp")),
        check_vma=False,
    )
```

```python
import math

import jax
import jax.numpy as jnp
from jax import lax
from jax.experimental import pallas as pl
from jax.experimental.pallas import tpu as pltpu
from jax.sharding import PartitionSpec as P

MESH = pl.DeviceIdType.MESH
HEAD = 128
NZ = 8
FOLD = 4
NEG = -1e30
EPS = 1e-06
CAP = 20
F32 = jnp.float32
BF16 = jnp.bfloat16


def place(x, z, c):
    return x * (2 * NZ) + lax.rem(z + 2 * NZ, NZ) * 2 + c


class Net:
    def __init__(self, send, recv):
        self.send_sems, self.recv_sems = send, recv
        cp = lax.axis_index("cp")
        self.cp = cp
        self.x = cp // (2 * NZ)
        self.z = (cp // 2) % NZ
        self.c = cp % 2
        self.f = lax.axis_index("fold")
        self.xp = 1 - self.x
        self.fp, self.fo, self.fm = [lax.rem(self.f + k, FOLD) for k in (1, 2, 3)]
        self.ids = {}
        self.sent = []

    def to(self, way):
        x, z, c = self.x, self.z, self.c
        if way == "z+":
            return {"cp": place(x, z + 1, c)}
        if way == "z-":
            return {"cp": place(x, z - 1, c)}
        if way == "x":
            return {"cp": place(1 - x, z, c)}
        if way == "c":
            return {"cp": place(x, z, 1 - c)}
        if way == "f+":
            return {"fold": self.fp}
        if way == "f-":
            return {"fold": self.fm}
        if way == "fo":
            return {"fold": self.fo}
        return {"section": 1 - lax.axis_index("section")}

    def greet(self, ways):
        for way in ways:
            pl.semaphore_signal(
                pltpu.get_barrier_semaphore(), inc=1, device_id=self.to(way), device_id_type=MESH
            )

    def meet(self, ways):
        pl.semaphore_wait(pltpu.get_barrier_semaphore(), len(ways))

    def slot(self, name):
        return self.ids.setdefault(name, len(self.ids))

    def copy(self, name, src, dst, way):
        i = self.slot(name)
        return pltpu.make_async_remote_copy(
            src_ref=src,
            dst_ref=dst,
            send_sem=self.send_sems.at[i],
            recv_sem=self.recv_sems.at[i],
            device_id=self.to(way),
            device_id_type=MESH,
        )

    def push(self, name, src, dst, way):
        copy = self.copy(name, src, dst, way)
        copy.start()
        self.sent.append((name[0], copy))

    def await_(self, name, dst, way):
        self.copy(name, dst, dst, way).wait_recv()

    def drain(self, *kinds):
        for kind, copy in self.sent:
            if not kinds or kind in kinds:
                copy.wait_send()
        self.sent = [entry for entry in self.sent if kinds and entry[0] not in kinds]


class Gather:
    def __init__(self, net, name, buf, rows1):
        self.net, self.name, self.buf = net, name, buf
        self.rows = buf.shape[1]
        self.rows1 = rows1

    def block(self, x, z, c, part="full"):
        ref = self.buf.at[place(x, z, c)]
        if part == "full":
            return ref
        if part == "r1":
            return ref.at[pl.ds(0, self.rows1)]
        return ref.at[pl.ds(self.rows1, self.rows - self.rows1)]

    def push(self, tag, key, way, part="full"):
        ref = self.block(*key, part)
        self.net.push((self.name, tag), ref, ref, way)

    def wait(self, tag, key, way, part="full"):
        self.net.await_((self.name, tag), self.block(*key, part), way)

    def tick(self, s):
        n = self.net
        x, z, c, xp, cp = n.x, n.z, n.c, n.xp, 1 - n.c
        if s == 0:
            for tag, way in (("zp0", "z+"), ("zm0", "z-"), ("x0", "x"), ("c0", "c")):
                self.push(tag, (x, z, c), way)
            return
        if s == 1:
            self.wait("x0", (xp, z, c), "x")
            self.push("yp0", (xp, z, c), "z+", "r2")
            self.push("ym0", (xp, z, c), "z-", "r2")
            self.push("cx0", (xp, z, c), "c")
        if s <= 4:
            near = "full" if s <= 3 else "r1"
            self.wait(f"zp{s - 1}", (x, z - s, c), "z+", near)
            if s <= 3:
                self.push(f"zp{s}", (x, z - s, c), "z+", "full" if s <= 2 else "r1")
                self.wait(f"zm{s - 1}", (x, z + s, c), "z-")
                self.push(f"zm{s}", (x, z + s, c), "z-", "full" if s <= 2 else "r2")
            self.push(f"xm{s}", (x, z - s, c), "x", "r1")
            if s <= 3:
                self.push(f"xp{s}", (x, z + s, c), "x", "r1")
            self.push(f"cm{s}", (x, z - s, c), "c", near)
            if s <= 3:
                self.push(f"cp{s}", (x, z + s, c), "c")
            else:
                self.wait("zm3", (x, z + 4, c), "z-", "r2")
                self.push("cn4", (x, z + 4, c), "c", "r2")
        if s >= 2 and s <= 5:
            d = s - 1
            self.wait(f"ym{d - 1}", (xp, z + d, c), "z-", "r2")
            if d <= 3:
                self.push(f"ym{d}", (xp, z + d, c), "z-", "r2")
                self.wait(f"yp{d - 1}", (xp, z - d, c), "z+", "r2")
                if d <= 2:
                    self.push(f"yp{d}", (xp, z - d, c), "z+", "r2")
            self.push(f"dp{d}", (xp, z + d, c), "c", "r2")
            if d <= 3:
                self.push(f"dm{d}", (xp, z - d, c), "c", "r2")
            self.wait(f"xm{d}", (xp, z - d, c), "x", "r1")
            self.push(f"em{d}", (xp, z - d, c), "c", "r1")
            if d <= 3:
                self.wait(f"xp{d}", (xp, z + d, c), "x", "r1")
                self.push(f"ep{d}", (xp, z + d, c), "c", "r1")

    def ready(self, d):
        n = self.net
        x, z, xp, cp = n.x, n.z, n.xp, 1 - n.c
        if d == 0:
            self.wait("c0", (x, z, cp), "c")
            self.wait("cx0", (xp, z, cp), "c")
            return
        side, s = ("p", d) if d > 0 else ("m", -d)
        self.wait(f"c{side}{s}", (x, z + d, cp), "c", "full" if s <= 3 else "r1")
        if s == 4:
            self.wait("cn4", (x, z + d, cp), "c", "r2")
        self.wait(f"d{'p' if s == 4 else side}{s}", (xp, z + d, cp), "c", "r2")
        self.wait(f"e{side}{s}", (xp, z + d, cp), "c", "r1")


DISTANCES = (0, -1, 1, -2, 2, -3, 3, -4)
STAGES = ((3, -4), (2, -3), (1, -2), (-1, 0))
WAYS = ("z+", "z-", "x", "c", "f+", "f-", "fo", "sec")
NT = (((1,), (1,)), ((), ()))


def layer(
    q, keys, values, segments, routes, weights, act, gain, wo, wg, wu, wd,
    passed, passed_segments,
    kvg, pool, xg, wgv, wuv, wdv, qs, top, total, mixed, attended, hits, rank, share, proj, mine, inbox, stat,
    slots, part, ra, rb, rc, rd, hidden, result, cin, xin, zin, yin, tin, resid, done,
    send, recv, pair_send, pair_recv, local,
):
    net = Net(send, recv)
    x, z, c, xp, cpeer = net.x, net.z, net.c, net.xp, 1 - net.c
    f, fp, fo, fm = net.f, net.fp, net.fo, net.fm
    tokens, feats = act.shape
    cap = 4 * CAP
    rows1 = tokens * 5 // 8
    rows2 = tokens - rows1
    net.greet(WAYS)

    kvg[net.cp, 0:tokens, 0:HEAD] = keys[...]
    kvg[net.cp, 0:tokens, HEAD:2 * HEAD] = values[...]
    weight = weights[...]
    coarse = weight.astype(BF16).astype(F32)
    side = jnp.broadcast_to(segments[...].astype(F32), (8, tokens))
    meta = jnp.concatenate([routes[...].astype(F32), coarse], axis=0)
    kvg[net.cp, tokens:tokens + 16, 0:HEAD] = meta.astype(BF16)
    meta = jnp.concatenate([weight - coarse, side], axis=0)
    kvg[net.cp, tokens:tokens + 16, HEAD:2 * HEAD] = meta.astype(BF16)
    eye = (
        lax.broadcasted_iota(jnp.int32, (tokens, tokens), 0) == lax.broadcasted_iota(jnp.int32, (tokens, tokens), 1)
    ).astype(F32).astype(BF16)
    seg_q = lax.dot_general(eye, jnp.concatenate([side, side], axis=0).astype(BF16), NT, preferred_element_type=F32)[:, 0:1]
    pool[net.cp] = lax.dot_general(eye, wo[...], NT, preferred_element_type=F32).astype(BF16)

    net.meet(WAYS)
    kv = Gather(net, "kv", kvg, rows1)
    out = Gather(net, "wo", pool, rows1)
    kv.tick(0)
    out.tick(0)
    hid = wg.shape[1]
    loads = [pltpu.make_async_copy(wd, wdv, local.at[2])]
    for k, (src, dst) in enumerate(((wg, wgv), (wu, wuv))):
        rows = pl.ds(f * hid, hid)
        loads.append(
            pltpu.make_async_copy(src.at[:, :, pl.ds(f * feats, feats)], dst.at[:, rows, :], local.at[k])
        )
    for copy in loads:
        copy.start()

    def resplit(k, src, dst):
        for way, t in (("f+", fp), ("f-", fm), ("fo", fo)):
            net.push(("w", k, way), src.at[:, :, pl.ds(t * feats, feats)], dst.at[:, pl.ds(f * hid, hid), :], way)

    resplit(0, wg, wgv)
    net.push(("seg",), segments, passed_segments, "sec")

    heads = q.shape[1] // HEAD
    for h in range(heads):
        qs[h] = q[:, h * HEAD:(h + 1) * HEAD]
    top[...] = jnp.full(top.shape, NEG, F32)
    total[...] = jnp.zeros(total.shape, F32)
    mixed[...] = jnp.zeros(mixed.shape, F32)
    factor = math.log2(math.e) / math.sqrt(HEAD)
    q_place = net.cp * tokens + lax.broadcasted_iota(jnp.int32, (tokens, 2 * tokens), 0)

    def attend(line, d):
        base = place(line, z + d, 0)
        ks = kvg[pl.ds(base, 2), 0:tokens, 0:HEAD].reshape(2 * tokens, HEAD)
        vs = kvg[pl.ds(base, 2), 0:tokens, HEAD:2 * HEAD].reshape(2 * tokens, HEAD)
        seg_k = jnp.concatenate(
            [kvg[base + i, tokens:tokens + 16, HEAD:2 * HEAD].astype(F32)[8:9] for i in range(2)], axis=1
        )
        k_place = base * tokens + lax.broadcasted_iota(jnp.int32, (tokens, 2 * tokens), 1)
        bias = jnp.where((k_place <= q_place) & (seg_k == seg_q), 0.0, NEG)
        score = lax.dot_general(qs[...].reshape(heads * tokens, HEAD), ks, NT, preferred_element_type=F32)
        score = score.reshape(heads, tokens, 2 * tokens) * factor + bias[None]
        old = top[...]
        new = jnp.maximum(old, jnp.max(score, axis=2, keepdims=True))
        terms = jnp.exp2(score - new[:, :, 0:1])
        fade = jnp.exp2(old - new)
        top[...] = new
        total[...] = total[...] * fade + jnp.sum(terms, axis=2, keepdims=True)
        more = jnp.dot(
            terms.astype(BF16).reshape(heads * tokens, 2 * tokens), vs, preferred_element_type=F32
        ).reshape(heads, tokens, HEAD)
        mixed[...] = mixed[...] * fade + more

    def attend_to(*distances):
        for d in distances:
            kv.ready(d)
            if d == 0:
                attend(x, 0)
                attend(xp, 0)
            else:
                attend(jnp.where(lax.rem(z + d + NZ, NZ) < z, x, 0), d)

    kv.tick(1)
    kv.tick(2)
    attend_to(0)
    kv.tick(3)
    out.tick(1)
    attend_to(-1, 1)
    kv.tick(4)
    out.tick(2)
    attend_to(-2, 2)
    kv.tick(5)
    attend_to(-3, 3)
    out.tick(3)
    attend_to(-4)
    for h in range(heads):
        attended[:, h * HEAD:(h + 1) * HEAD] = (mixed[h] / total[h]).astype(BF16)

    pairs = [(line, d) for d in DISTANCES for line in range(2)]
    per = 4 * NZ // FOLD
    two = 2 * tokens

    def owner(line, d):
        base = place(line, z + d, 0)
        t = base // per
        return base, lax.rem(t - f + FOLD, FOLD), base % per

    def shipment(n, line, d):
        base, k, column = owner(line, d)
        return pltpu.make_async_remote_copy(
            src_ref=proj.at[n],
            dst_ref=inbox.at[k - 1, :, pl.ds(pl.multiple_of(column * tokens, two), two)],
            send_sem=pair_send.at[n],
            recv_sem=pair_recv.at[(k - 1) * 4 + column // 2],
            device_id={"fold": base // per},
            device_id_type=MESH,
        )

    def project_to(*distances):
        for d in distances:
            out.ready(d)
            for line in range(2):
                n = pairs.index((line, d))
                base, k, column = owner(line, d)
                rhs = pool[pl.ds(base, 2)].reshape(two, attended.shape[1])
                res = lax.dot_general(attended[...], rhs, NT, preferred_element_type=F32).astype(BF16)
                proj[n] = res

                @pl.when(k == 0)
                def _():
                    mine[:, pl.ds(pl.multiple_of(column * tokens, two), two)] = res

                @pl.when(k != 0)
                def _():
                    shipment(n, line, d).start()

    project_to(0, -1, 1)
    out.tick(4)
    project_to(-2, 2)
    out.tick(5)
    project_to(-3, 3, -4)
    base = act[...].astype(F32) + mine[...].astype(F32)
    for k in range(3):
        for j in range(4):
            block = inbox.at[k, :, pl.ds(j * two, two)]
            pltpu.make_async_remote_copy(
                src_ref=block,
                dst_ref=block,
                send_sem=pair_send.at[0],
                recv_sem=pair_recv.at[k * 4 + j],
                device_id={"fold": fp},
                device_id_type=MESH,
            ).wait_recv()
        base = base + inbox[k].astype(F32)
    kept = base.astype(BF16)
    resid[...] = kept
    wide = kept.astype(F32)
    stat[0] = lax.dot_general(
        jnp.ones((8, feats), F32), wide * wide, NT, preferred_element_type=F32, precision=lax.Precision.HIGHEST
    )
    for k, way in enumerate(("f+", "f-", "fo")):
        net.push(("s", k), stat.at[0], stat.at[k + 1], way)
    normed = wide * gain[...].astype(F32)
    for k, way in enumerate(("f+", "f-", "fo")):
        net.await_(("s", k), stat.at[k + 1], way)
    squares = stat[0] + stat[1] + stat[2] + stat[3]
    scale = lax.rsqrt(squares / (feats * FOLD) + EPS)
    scale = lax.dot_general(eye.astype(F32), scale, NT, preferred_element_type=F32, precision=lax.Precision.HIGHEST)
    xg[net.cp] = (normed * scale[:, 0:1]).astype(BF16)

    xs = Gather(net, "x", xg, rows1)
    xs.tick(0)
    resplit(1, wu, wuv)

    for g in range(NZ):
        for e in range(2):
            expert = (2 * net.cp + e).astype(F32)
            for k in range(4):
                meta = kvg[place(k // 2, g, k % 2), tokens:tokens + 16].astype(F32)
                chosen = meta[0:8, 0:tokens] == expert
                row = pl.ds(2 * g + e, 1)
                columns = pl.ds(k * tokens, tokens)
                hits[row, columns] = jnp.sum(jnp.where(chosen, 1.0, 0.0), axis=0, keepdims=True)
                shares = meta[8:16, 0:tokens] + meta[0:8, tokens:2 * tokens]
                share[row, columns] = jnp.sum(jnp.where(chosen, shares, 0.0), axis=0, keepdims=True)
    xs.tick(1)
    wide4 = 4 * tokens
    earlier = lax.broadcasted_iota(jnp.int32, (wide4, wide4), 0) < lax.broadcasted_iota(jnp.int32, (wide4, wide4), 1)
    hit = hits[...]
    before = jnp.dot(hit.astype(BF16), jnp.where(earlier, 1.0, 0.0).astype(BF16), preferred_element_type=F32)
    rank[...] = jnp.where(hit > 0.5, before, -1.0)

    def group(d):
        return lax.rem(z + d + NZ, NZ)

    def pick(d, e):
        row = rank[pl.ds(2 * group(d) + e, 1), :]
        want = lax.broadcasted_iota(jnp.int32, (cap, 4 * tokens), 0).astype(F32)
        return jnp.where(want == row, 1.0, 0.0)

    def select(i):
        for j, d in enumerate(STAGES[i]):
            xs.ready(d)
            g = group(d)
            low = xg[pl.ds(2 * g, 2)].reshape(2 * tokens, feats)
            high = xg[pl.ds(2 * NZ + 2 * g, 2)].reshape(2 * tokens, feats)
            choice = jnp.concatenate([pick(d, 0), pick(d, 1)], axis=0).astype(BF16)
            got = jnp.dot(choice[:, 0:2 * tokens], low, preferred_element_type=F32)
            got = (got + jnp.dot(choice[:, 2 * tokens:], high, preferred_element_type=F32)).astype(BF16)
            for e in range(2):
                slots[i, pl.ds((2 * e + j) * cap, cap), :] = got[e * cap:(e + 1) * cap]

    wide_hid = FOLD * hid

    def enter(i, k):
        w = (wgv, wuv)[k]
        columns = pl.ds(k * wide_hid, wide_hid)
        for e in range(2):
            lhs = slots[i, pl.ds(2 * e * cap, 2 * cap), :]
            res = lax.dot_general(lhs, w[e], NT, preferred_element_type=F32).astype(BF16)
            part[i, 2 * e, :, columns] = res[0:cap]
            part[i, 2 * e + 1, :, columns] = res[cap:]

    def gate(i):
        enter(i, 0)

    def up(i):
        enter(i, 1)
        net.push(("a", i), part.at[i, fo, :, pl.ds(0, wide_hid)], ra.at[i], "f+")
        net.push(("b", i), part.at[i, fo, :, pl.ds(wide_hid, wide_hid)], rb.at[i], "f-")

    def have(k):
        dst = (wgv, wuv)[k]
        for way, t in (("f+", fm), ("f-", fp), ("fo", fo)):
            net.await_(("w", k, way), dst.at[:, pl.ds(t * hid, hid), :], way)
        loads[k + 1].wait()

    def relay(i):
        left, right = pl.ds(0, wide_hid), pl.ds(wide_hid, wide_hid)
        net.await_(("a", i), ra.at[i], "f+")
        part[i, fp, :, left] = (part[i, fp, :, left].astype(F32) + ra[i].astype(F32)).astype(BF16)
        net.push(("c", i), part.at[i, fp], rc.at[i], "f+")
        net.await_(("b", i), rb.at[i], "f-")
        part[i, fm, :, right] = (part[i, fm, :, right].astype(F32) + rb[i].astype(F32)).astype(BF16)
        net.push(("d", i), part.at[i, fm], rd.at[i], "f-")

    def activate(i):
        net.await_(("c", i), rc.at[i], "f+")
        net.await_(("d", i), rd.at[i], "f-")
        both = part[i, f].astype(F32) + rc[i].astype(F32) + rd[i].astype(F32)
        gate, up = both[:, 0:wide_hid], both[:, wide_hid:2 * wide_hid]
        hidden[i, f] = (gate / (1.0 + jnp.exp(-gate)) * up).astype(BF16)
        net.push(("h+", i), hidden.at[i, f], hidden.at[i, f], "f+")
        net.push(("h-", i), hidden.at[i, f], hidden.at[i, f], "f-")

    half_hid = wide_hid // 2

    def spread(i):
        net.await_(("h+", i), hidden.at[i, fm], "f+")
        lower = hidden.at[i, fm, :, pl.ds(0, half_hid)]
        net.push(("i+", i), lower, lower, "f+")
        net.await_(("h-", i), hidden.at[i, fp], "f-")
        upper = hidden.at[i, fp, :, pl.ds(half_hid, half_hid)]
        net.push(("i-", i), upper, upper, "f-")

    def leave(i):
        net.await_(("i+", i), hidden.at[i, fo, :, pl.ds(0, half_hid)], "f+")
        net.await_(("i-", i), hidden.at[i, fo, :, pl.ds(half_hid, half_hid)], "f-")
        for group_ids in ((0, 1),) if i < 3 else ((0,), (1,)):
            for e in range(2):
                lhs = hidden[i, pl.ds(2 * e + group_ids[0], len(group_ids))].reshape(len(group_ids) * cap, wide_hid)
                res = jnp.dot(lhs, wdv[e], preferred_element_type=F32)
                for n, j in enumerate(group_ids):
                    d = STAGES[i][j]
                    row = share[pl.ds(2 * group(d) + e, 1), :]
                    scaled = jnp.sum(pick(d, e) * row, axis=1, keepdims=True)
                    result[2 * j + e] = (res[n * cap:(n + 1) * cap] * scaled).astype(BF16)
            for j in group_ids:
                d = STAGES[i][j]
                g = group(d)
                choice = jnp.concatenate([pick(d, 0), pick(d, 1)], axis=0).astype(BF16)
                res = result[2 * j:2 * j + 2].reshape(2 * cap, feats)
                summed = lax.dot_general(
                    choice, res, (((0,), (0,)), ((), ())), preferred_element_type=F32
                ).astype(BF16)
                for k in range(4):
                    pool[place(k // 2, g, k % 2)] = summed[k * tokens:(k + 1) * tokens]
                for xx in range(2):
                    net.push(("rc", d, xx), pool.at[place(xx, g, cpeer)], cin.at[g, xx], "c")

    def accumulate(at, rows, inc):
        pool[at, rows] = (pool[at, rows].astype(F32) + inc.astype(F32)).astype(BF16)

    full, ahead, rest = pl.ds(0, tokens), pl.ds(0, rows1), pl.ds(rows1, rows2)

    def merge(*distances):
        for d in distances:
            g = group(d)
            for xx in range(2):
                net.await_(("rc", d, xx), cin.at[g, xx], "c")
                accumulate(place(xx, g, c), full, cin[g, xx])
            net.push(("rx", d), pool.at[place(xp, g, c), ahead], xin.at[g], "x")

    def cross(d):
        g = group(d)
        net.await_(("rx", d), xin.at[g], "x")
        accumulate(place(x, g, c), ahead, xin[g])

    lines = (
        ("z-", -1, 4, x, zin, 0, ahead),
        ("z+", 1, 3, x, zin, 4, ahead),
        ("z-", -1, 3, x, yin, 0, rest),
        ("z+", 1, 4, x, yin, 3, rest),
        ("z-", -1, 3, xp, yin, 7, rest),
        ("z+", 1, 4, xp, yin, 10, rest),
    )

    def hop(k, d):
        way, sign, hops, line, inbox, first, rows = lines[k]
        s = hops - abs(d)
        at = place(line, z + d, c)
        if s > 0:
            net.await_(("rz", k, s - 1), inbox.at[first + s - 1], way)
            accumulate(at, rows, inbox[first + s - 1])
        if s < hops:
            net.push(("rz", k, s), pool.at[at, rows], inbox.at[first + s], way)

    xs.tick(2)
    have(0)
    xs.tick(3)
    select(3)
    gate(3)
    xs.tick(4)
    select(2)
    gate(2)
    xs.tick(5)
    select(1)
    gate(1)
    select(0)
    net.drain("wo")
    gate(0)
    have(1)
    loads[0].wait()
    up(0)
    up(1)
    relay(0)
    relay(1)
    activate(0)
    up(2)
    activate(1)
    spread(0)
    relay(2)
    leave(0)
    spread(1)
    up(3)
    activate(2)
    merge(-4, 3)
    hop(3, 4)
    hop(5, 4)
    leave(1)
    relay(3)
    spread(2)
    cross(-4)
    hop(0, -4)
    cross(3)
    hop(1, 3)
    merge(-3, 2)
    hop(2, -3)
    hop(4, -3)
    activate(3)
    leave(2)
    hop(3, 3)
    hop(5, 3)
    cross(-3)
    hop(0, -3)
    cross(2)
    spread(3)
    hop(1, 2)
    merge(-2, 1)
    hop(2, -2)
    hop(4, -2)
    hop(3, 2)
    hop(5, 2)
    leave(3)
    cross(1)
    cross(-2)
    hop(0, -2)
    hop(1, 1)
    hop(3, 1)
    hop(5, 1)
    merge(-1)
    hop(2, -1)
    hop(4, -1)
    cross(-1)
    hop(0, -1)
    merge(0)
    hop(5, 0)
    hop(4, 0)
    net.push(("rt",), pool.at[place(xp, z, c), rest], tin, "x")
    hop(3, 0)
    hop(2, 0)
    cross(0)
    hop(1, 0)
    hop(0, 0)
    own = resid[...].astype(F32) + pool[net.cp].astype(F32)
    done[ahead] = own[0:rows1].astype(BF16)
    net.push(("out", 0), done.at[ahead], passed.at[ahead], "sec")
    net.await_(("rt",), tin, "x")
    done[rest] = (own[rows1:] + tin[...].astype(F32)).astype(BF16)
    net.push(("out", 1), done.at[rest], passed.at[rest], "sec")
    net.await_(("seg",), passed_segments, "sec")
    net.await_(("out", 0), passed.at[ahead], "sec")
    net.await_(("out", 1), passed.at[rest], "sec")
    net.drain()
    for n, (line, d) in enumerate(pairs):
        @pl.when(owner(line, d)[1] != 0)
        def _():
            shipment(n, line, d).wait_send()


def run_layer(q, keys, values, segments, routes, weights, act, gain, wo, wg, wu, wd):
    tokens, feats = act.shape
    blocks = 4 * NZ
    experts, quarter, wide = wg.shape
    hid = quarter * FOLD
    cap = 4 * CAP
    heads = q.shape[1] // HEAD
    rows1 = tokens * 5 // 8
    dma = pltpu.SemaphoreType.DMA

    def scratch(*shape, dtype=BF16):
        return pltpu.VMEM(shape, dtype)

    vmem, hbm = pl.BlockSpec(memory_space=pltpu.VMEM), pl.BlockSpec(memory_space=pl.ANY)
    return pl.pallas_call(
        layer,
        out_shape=(jax.ShapeDtypeStruct((tokens, feats), BF16), jax.ShapeDtypeStruct(segments.shape, segments.dtype)),
        in_specs=[vmem] * 9 + [hbm] * 3,
        out_specs=(vmem, vmem),
        scratch_shapes=[
            scratch(blocks, tokens + 16, 2 * HEAD),
            scratch(blocks, tokens, feats),
            scratch(blocks, tokens, feats),
            scratch(experts, hid, feats),
            scratch(experts, hid, feats),
            scratch(experts, hid, feats),
            scratch(heads, tokens, HEAD),
            scratch(heads, tokens, HEAD, dtype=F32),
            scratch(heads, tokens, HEAD, dtype=F32),
            scratch(heads, tokens, HEAD, dtype=F32),
            scratch(*q.shape),
            scratch(2 * NZ, 4 * tokens, dtype=F32),
            scratch(2 * NZ, 4 * tokens, dtype=F32),
            scratch(2 * NZ, 4 * tokens, dtype=F32),
            scratch(2 * NZ, tokens, 2 * tokens),
            scratch(tokens, feats),
            scratch(3, tokens, feats),
            scratch(4, 8, tokens, dtype=F32),
            scratch(4, 4 * cap, feats),
            scratch(4, FOLD, cap, 2 * hid),
            scratch(4, cap, hid),
            scratch(4, cap, hid),
            scratch(4, cap, 2 * hid),
            scratch(4, cap, 2 * hid),
            scratch(4, FOLD, cap, hid),
            scratch(4, cap, feats),
            scratch(NZ, 2, tokens, feats),
            scratch(NZ, rows1, feats),
            scratch(7, rows1, feats),
            scratch(14, tokens - rows1, feats),
            scratch(tokens - rows1, feats),
            scratch(tokens, feats),
            scratch(tokens, feats),
            dma((240,)),
            dma((240,)),
            dma((2 * NZ,)),
            dma((12,)),
            dma((3,)),
        ],
        compiler_params=pltpu.CompilerParams(collective_id=0, has_side_effects=True, vmem_limit_bytes=62 * 2**20),
        name="layer",
    )(q, keys, values, segments, routes, weights, act, gain, wo, wg, wu, wd)


def body(
    activations, queries, keys, values, segments, routes, route_weight, norm_gain, w_out, w_gate, w_up, w_down,
):
    passed, moved = run_layer(
        queries[0], keys[0], values[0], segments, routes[0].T, route_weight[0].T, activations[0], norm_gain,
        w_out[0], w_gate[0], w_up[0], w_down[0],
    )
    return passed[None], moved


def solution(mesh):
    return jax.shard_map(
        body,
        mesh=mesh,
        in_specs=(
            P("section", "cp", "fold"),
            P("section", "cp", "fold"),
            P("section", "cp", "fold"),
            P("section", "cp", "fold"),
            P("section", "cp"),
            P("section", "cp", None),
            P("section", "cp", None),
            P("section", "fold"),
            P("section", "fold", "cp"),
            P("section", "cp", "fold", None),
            P("section", "cp", "fold", None),
            P("section", "cp", None, "fold"),
        ),
        out_specs=(P("section", "cp", "fold"), P("section", "cp")),
        check_vma=False,
    )
```
